256 devices in a mesh: comp: 32 (over x, z_lo, core), space: 8 (over z_hi, y).
Axes of the slice: x: 4, y: 4, z: 8 (z_hi: 2, z_lo: 4; z = z_hi * 4 + z_lo), core: 2. Of those that a mesh axis runs over, the one named last changes fastest.
Arguments:
- spectrum: float32 [1152, 131072], P(None, ('comp', 'space')), may hold values from 0.05 to 1
- wind_field: float32 [2, 131072], P(None, ('comp', 'space')), may hold values from -4 to 4
- coupling: bfloat16 [1152, 1152], replicated, may hold values from -0.1875 to 0.1875
- growth: float32 [32], replicated, may hold values from 0.02 to 0.2
- dissipation: float32 [32], replicated, may hold values from 0.1 to 1
- group_speed: float32 [32, 32], replicated, may hold values from 0.1 to 0.45
- refraction: float32 [32, 32], replicated, may hold values from -0.5 to 0.5
- depths: float32 [32], replicated, may hold values from 0.1 to 1
- sea_mask: int32 [1024, 128], P('space'), may hold values 0 or 1
- depth_index: int32 [1024, 128], P('space'), may hold values from 0 to 31
Outputs:
- spectrum_out: float32 [1152, 131072], P(None, ('comp', 'space'))
The draws below stay inside these ranges and needn't reach their ends.
All inputs are finite; a program needn't handle non-finite values. No bound on the sum of `sea_mask` on one device may be relied on, other than what follows from the above.
Results may differ from the reference program's by a relative error of at most 0.00051.
Values sent between devices are 32-bit elements; how exact they have to be, the bound alone decides.
A program may use at most 64 MiB of HBM per device.

```python
import math
import jax
import jax.numpy as jnp
from jax import lax

NF = 32
ND = 36
K = 1152
NDEP = 32
RB = 4
NY = 128
SUBSTEPS = 3
NX = 1024
POINTS = 131072
N_COMP = 32
N_SPACE = 8


def with_ends(result, own_key, least, largest):
    dims = result.shape
    place = [jax.random.randint(jax.random.fold_in(own_key, axis), (), 0, dims[axis]) for axis in range(len(dims))]
    result = result.at[tuple(place)].set(least)
    longest = dims.index(max(dims))
    place[longest] = (place[longest] + 1) % dims[longest]
    return result.at[tuple(place)].set(largest)


def steps_of(rng, dims, pieces, smallest, top_value):
    def one(axis_at, parts):
        steps = jax.random.uniform(jax.random.fold_in(jax.random.fold_in(rng, 6), axis_at), (parts,), jnp.float32, smallest / len(pieces), top_value / len(pieces))
        return jnp.repeat(jnp.exp(steps), dims[axis_at] // parts).reshape((-1,) + (1,) * (len(dims) - axis_at - 1))

    loudness = one(*pieces[0])
    for cut in pieces[1:]:
        loudness = loudness * one(*cut)
    return loudness


def normal_values(stream_key, dims, scale, most, split=(), held_as=jnp.bfloat16):
    loudness = steps_of(stream_key, dims, split, -0.22, 0.18) if split else 1.0
    result = jax.random.normal(stream_key, dims, jnp.float32) * scale * loudness
    return jnp.minimum(jnp.maximum(result, -most), most).astype(held_as)


def setup_inputs(seed: int = 0) -> dict:
    keys = jax.random.split(jax.random.key(seed), 11)
    spectrum = jnp.clip(jnp.exp(math.log(1.0) - 2.9957323 * jax.random.uniform(keys[0], (K, POINTS), jnp.float32) ** steps_of(keys[0], (K, POINTS), ((1, 256),), -0.2, 0.2)), 0.05, 1.0)
    wind_field = normal_values(keys[1], (2, POINTS), 1.0, 4.0, ((1, 256),), jnp.float32)
    coupling = normal_values(keys[2], (K, K), K ** -0.5, 0.1875)
    growth = jnp.clip(jnp.exp(jax.random.uniform(keys[3], (NF,), jnp.float32, math.log(0.02), math.log(0.2))), 0.02, 0.2)
    dissipation = jnp.clip(jnp.exp(jax.random.uniform(keys[4], (NF,), jnp.float32, math.log(0.1), math.log(1.0))), 0.1, 1.0)
    group_speed = jnp.clip(jnp.exp(jax.random.uniform(keys[5], (NF, NDEP), jnp.float32, math.log(0.1), math.log(0.45))), 0.1, 0.45)
    refraction = jnp.clip(jax.random.uniform(keys[6], (NF, NDEP), jnp.float32, -0.5, 0.5), -0.5, 0.5)
    depths = jnp.clip(jax.random.uniform(keys[7], (NDEP,), jnp.float32, 0.1, 1.0), 0.1, 1.0)
    sea_mask = with_ends((jax.random.randint(keys[8], (NX, NY), 0, 10) < 9).astype(jnp.int32), jax.random.fold_in(keys[8], 1), 0, 1)
    depth_index = with_ends(jax.random.randint(keys[9], (NX, NY), 0, NDEP), jax.random.fold_in(keys[9], 1), 0, NDEP - 1).astype(jnp.int32)
    return {"spectrum": spectrum, "wind_field": wind_field, "coupling": coupling, "growth": growth, "dissipation": dissipation, "group_speed": group_speed, "refraction": refraction, "depths": depths, "sea_mask": sea_mask, "depth_index": depth_index}


def direction_angles():
    return 2.0 * jnp.pi * jnp.arange(ND, dtype=jnp.float32) / ND


def source_terms(energy, wind_block, coupling, growth, dissipation):
    nfreq = growth.shape[0]
    angles = direction_angles()
    projected = jnp.cos(angles)[:, None] * wind_block[0][None, :] + jnp.sin(angles)[:, None] * wind_block[1][None, :]
    forcing = jnp.maximum(projected, 0.0)
    driving = growth[:, None, None] * (forcing * forcing)[None]
    average = jnp.mean(energy, axis=0)
    damping = dissipation[:, None, None] * (average / (average + 1.0))[None, None, :]
    nonlinear = jnp.dot(coupling, energy.astype(jnp.bfloat16), preferred_element_type=jnp.float32)
    shaped = energy.reshape(nfreq, ND, -1)
    return (shaped + (driving - damping) * shaped).reshape(energy.shape) + 0.25 * nonlinear


def face_flux(behind, centre, forward, beyond, courant):
    central = 0.5 * (centre + forward) - 0.5 * courant * (forward - centre)
    curvature = jnp.where(courant >= 0.0, forward - 2.0 * centre + behind, beyond - 2.0 * forward + centre)
    return courant * (central - (1.0 - courant * courant) / 6.0 * curvature)


def cut_along(values, offset, length, along):
    return lax.slice_in_dim(values, offset, offset + length, axis=along)


def advect(padded, speeds, weight, along):
    inner_count = padded.shape[along] - 4
    courant = 0.5 * (cut_along(speeds, 1, inner_count + 1, along) + cut_along(speeds, 2, inner_count + 1, along))
    if weight is not None:
        courant = courant * cut_along(weight, 1, inner_count + 1, along) * cut_along(weight, 2, inner_count + 1, along)
    face_values = face_flux(cut_along(padded, 0, inner_count + 1, along), cut_along(padded, 1, inner_count + 1, along),
                            cut_along(padded, 2, inner_count + 1, along), cut_along(padded, 3, inner_count + 1, along), courant)
    return cut_along(padded, 2, inner_count, along) - (cut_along(face_values, 1, inner_count, along) - cut_along(face_values, 0, inner_count, along))


def pad_zero(values, along, width):
    padding = [(0, 0)] * values.ndim
    padding[along] = (width, width)
    return jnp.pad(values, padding)


def wrap_dirs(values, along):
    length = values.shape[along]
    return jnp.concatenate([cut_along(values, length - 2, 2, along), values, cut_along(values, 0, 2, along)], axis=along)


def surface_slopes(height):
    rows_padded = jnp.pad(height, ((1, 1), (0, 0)))
    cols_padded = jnp.pad(height, ((0, 0), (1, 1)))
    return 0.5 * (rows_padded[2:] - rows_padded[:-2]), 0.5 * (cols_padded[:, 2:] - cols_padded[:, :-2])


def transport_speeds(speed_pts, refract_pts, height):
    angles = direction_angles()
    cosine_dir = jnp.cos(angles)[:, None, None]
    sine_dir = jnp.sin(angles)[:, None, None]
    slope_x, slope_y = surface_slopes(height)
    speed_wide = jnp.expand_dims(speed_pts, -3)
    speed_x = speed_wide * cosine_dir
    speed_y = speed_wide * sine_dir
    speed_dir = jnp.expand_dims(refract_pts, -3) * (sine_dir * slope_x - cosine_dir * slope_y)
    return speed_x, speed_y, speed_dir


def cross_passes(energy, speed_y, speed_dir, mask_wide):
    y_axis = energy.ndim - 1
    dir_axis = energy.ndim - 3
    energy = advect(pad_zero(energy, y_axis, 2), pad_zero(speed_y, y_axis, 2), pad_zero(mask_wide, y_axis, 2), y_axis)
    energy = advect(wrap_dirs(energy, dir_axis), wrap_dirs(speed_dir, dir_axis), None, dir_axis)
    return energy * mask_wide


def reference(spectrum, wind_field, coupling, growth, dissipation, group_speed, refraction, depths, sea_mask, depth_index):
    block_count = N_COMP * N_SPACE
    block_points = RB * NY
    blocks = jnp.moveaxis(spectrum.reshape(K, block_count, block_points), 1, 0)
    wind_blocks = jnp.moveaxis(wind_field.reshape(2, block_count, block_points), 1, 0)
    sourced = lax.map(lambda paired: source_terms(paired[0], paired[1], coupling, growth, dissipation), (blocks, wind_blocks))
    grid_energy = sourced.reshape(N_COMP, N_SPACE, NF, ND, RB, NY).transpose(2, 3, 1, 0, 4, 5).reshape(NF, ND, NX, NY)
    mask_float = sea_mask.astype(jnp.float32)
    height = depths[depth_index] * mask_float
    mask_wide = mask_float[None]

    def one_freq(freq_item):
        energy, speed_row, refract_row = freq_item
        speed_x, speed_y, speed_dir = transport_speeds(speed_row[depth_index], refract_row[depth_index], height)
        for substep in range(SUBSTEPS):
            energy = advect(pad_zero(energy, 1, 2), pad_zero(speed_x, 1, 2), pad_zero(mask_wide, 1, 2), 1)
            energy = cross_passes(energy, speed_y, speed_dir, mask_wide)
        return energy

    moved = lax.map(one_freq, (grid_energy, group_speed, refraction))
    return moved.reshape(NF, ND, N_SPACE, N_COMP, RB, NY).transpose(0, 1, 3, 2, 4, 5).reshape(K, POINTS)
```

```python
import functools

import jax
import jax.numpy as jnp
import numpy as np
from jax import lax
from jax.experimental import pallas as pl
from jax.experimental.pallas import tpu as pltpu
from jax.sharding import PartitionSpec as P

ND = 36
NQ = 9
RB = 4
NY = 128
SUBSTEPS = 3
FB = 8
SLOTS = 6 * NQ
MESH = pl.DeviceIdType.MESH


def direction_tables():
    angles = np.float32(2.0 * np.pi) * np.arange(ND, dtype=np.float32) / np.float32(ND)
    cosine = np.cos(angles.astype(np.float64)).astype(np.float32)
    sine = np.sin(angles.astype(np.float64)).astype(np.float32)
    half_cos = np.float32(0.5) * (cosine + np.roll(cosine, -1))
    half_sin = np.float32(0.5) * (sine + np.roll(sine, -1))
    return np.concatenate([cosine, sine, half_cos, half_sin])


def face_of(nu, base, diff, second):
    return nu * (base + (1.0 - nu) * (0.5 * diff - (nu * (1.0 / 6.0) + (1.0 / 6.0)) * second))


def kernel(
    nfreq,
    ncomp,
    nspace,
    trig,
    growth,
    dissipation,
    depths,
    wind,
    group_speed,
    refraction,
    sea_mask,
    depth_index,
    spectrum,
    coupling,
    out,
    spec_v,
    coup_v,
    spec_b,
    nonlin,
    energy,
    work,
    out_v,
    send_l,
    send_r,
    recv_l,
    recv_r,
    coast_out,
    coast_in,
    gx,
    gy,
    rx,
    ry,
    mask_v,
    wind_v,
    ratio_v,
    load_sem,
    coup_sem,
    store_sem,
    send_l_sem,
    send_r_sem,
    recv_l_sem,
    recv_r_sem,
    coast_send_sem,
    coast_recv_sem,
):
    blocks = nfreq // FB
    rows_b = FB * ND
    components = nfreq * ND
    c = lax.axis_index("comp")
    s = lax.axis_index("space")
    total = ncomp * nspace
    n = s * ncomp + c
    before = lax.rem(n + total - 1, total)
    after = lax.rem(n + 1, total)
    left = (lax.rem(before, ncomp), lax.div(before, ncomp))
    right = (lax.rem(after, ncomp), lax.div(after, ncomp))
    edge_l = jnp.where(n > 0, 1.0, 0.0).astype(jnp.float32)
    edge_r = jnp.where(n < total - 1, 1.0, 0.0).astype(jnp.float32)

    barrier = pltpu.get_barrier_semaphore()
    pl.semaphore_signal(barrier, inc=1, device_id=left, device_id_type=MESH)
    pl.semaphore_signal(barrier, inc=1, device_id=right, device_id_type=MESH)

    def lanes(r):
        return slice(r * NY, (r + 1) * NY)

    def spec_load(r):
        return pltpu.make_async_copy(spectrum.at[:, lanes(r)], spec_v.at[r], load_sem.at[r])

    for r in range(RB):
        spec_load(r).start()

    def coup_load(b):
        rows = pl.ds(pl.multiple_of(b * rows_b, rows_b), rows_b)
        return pltpu.make_async_copy(coupling.at[rows], coup_v.at[rows], coup_sem.at[b])

    for b in range(blocks):
        coup_load(b).start()

    own_mask = [sea_mask[pl.ds(c * RB + r, 1), :] for r in range(RB)]
    own_index = [depth_index[pl.ds(c * RB + r, 1), :] for r in range(RB)]
    for side, r in ((0, 0), (1, RB - 1)):
        coast_out[side, 0] = jnp.broadcast_to(own_mask[r], (8, NY))
        coast_out[side, 1] = jnp.broadcast_to(own_index[r], (8, NY))

    pl.semaphore_wait(barrier, 2)

    def coast_copy(side):
        return pltpu.make_async_remote_copy(
            src_ref=coast_out.at[side],
            dst_ref=coast_in.at[1 - side],
            send_sem=coast_send_sem.at[side],
            recv_sem=coast_recv_sem.at[1 - side],
            device_id=left if side == 0 else right,
            device_id_type=MESH,
        )

    for side in range(2):
        coast_copy(side).start()

    def to_left(k):
        return pltpu.make_async_remote_copy(
            src_ref=send_l.at[k],
            dst_ref=recv_r.at[k],
            send_sem=send_l_sem.at[k],
            recv_sem=recv_r_sem.at[k],
            device_id=left,
            device_id_type=MESH,
        )

    def to_right(k):
        return pltpu.make_async_remote_copy(
            src_ref=send_r.at[k],
            dst_ref=recv_l.at[k],
            send_sem=send_r_sem.at[k],
            recv_sem=recv_l_sem.at[k],
            device_id=right,
            device_id_type=MESH,
        )

    for r in range(RB):
        spec_load(r).wait()

        def cast_rows(i, acc, r=r):
            rows = pl.ds(pl.multiple_of(i * 64, 64), 64)
            block = spec_v[r, rows, :]
            spec_b[rows, lanes(r)] = block.astype(jnp.bfloat16)
            return acc + jnp.sum(block.reshape(8, 8, NY), axis=0)

        acc = lax.fori_loop(0, components // 64, cast_rows, jnp.zeros((8, NY), jnp.float32))
        average = jnp.sum(acc, axis=0, keepdims=True) * (1.0 / components)
        ratio_v[:, lanes(r)] = jnp.broadcast_to(average / (average + 1.0), (8, NY))
    wind_v[0] = jnp.broadcast_to(wind[0:1, :], (8, RB * NY))
    wind_v[1] = jnp.broadcast_to(wind[1:2, :], (8, RB * NY))

    for side in range(2):
        coast_copy(side).wait()
    mask_rows = (
        [coast_in[0, 0, 0:1, :].astype(jnp.float32) * edge_l]
        + [m.astype(jnp.float32) for m in own_mask]
        + [coast_in[1, 0, 0:1, :].astype(jnp.float32) * edge_r]
    )
    index_rows = [coast_in[0, 1, 0:1, :]] + own_index + [coast_in[1, 1, 0:1, :]]
    levels = depths.shape[0]
    level = lax.broadcasted_iota(jnp.int32, (levels, NY), 0)
    onehot = jnp.concatenate(
        [(jnp.broadcast_to(row, (levels, NY)) == level).astype(jnp.float32) for row in index_rows], axis=1
    )
    speeds = jnp.dot(
        group_speed[...], onehot, precision=lax.Precision.HIGHEST, preferred_element_type=jnp.float32
    )
    turning = jnp.dot(
        refraction[...],
        onehot[:, NY : (RB + 1) * NY],
        precision=lax.Precision.HIGHEST,
        preferred_element_type=jnp.float32,
    )
    lane_row = lax.broadcasted_iota(jnp.int32, (1, NY), 1)
    heights = []
    for row, mask in zip(index_rows, mask_rows):
        height = jnp.zeros((1, NY), jnp.float32)
        for entry in range(levels):
            height = jnp.where(row == entry, depths[entry], height)
        heights.append(height * mask)
    for j in range(RB + 1):
        pair = 0.5 * (speeds[:, lanes(j)] + speeds[:, lanes(j + 1)])
        gx[j] = pair * (mask_rows[j] * mask_rows[j + 1])
    for r in range(RB):
        mask = mask_rows[r + 1]
        own = speeds[:, lanes(r + 1)]
        beyond = jnp.where(lane_row == NY - 1, 0.0, pltpu.roll(jnp.broadcast_to(mask, (8, NY)), NY - 1, 1)[:1])
        gy[r] = 0.5 * (own + pltpu.roll(own, NY - 1, 1)) * (mask * beyond)
        wide = jnp.broadcast_to(heights[r + 1], (8, NY))
        up = jnp.where(lane_row == NY - 1, 0.0, pltpu.roll(wide, NY - 1, 1)[:1])
        down = jnp.where(lane_row == 0, 0.0, pltpu.roll(wide, 1, 1)[:1])
        rx[r] = turning[:, lanes(r)] * (0.5 * (heights[r + 2] - heights[r]))
        ry[r] = turning[:, lanes(r)] * (0.5 * (up - down))
        mask_v[r] = jnp.broadcast_to(mask, (8, NY))

    def pack(q, i, k, rows):
        if q in (0, 3):
            at = i + (0 if q == 0 else NQ)
            send_r[k, 2 * at] = rows[RB - 2]
            send_r[k, 2 * at + 1] = rows[RB - 1]
            send_l[k, 4 * NQ + at] = rows[0]
        else:
            at = i + (0 if q == 1 else NQ)
            send_l[k, 2 * at] = rows[0]
            send_l[k, 2 * at + 1] = rows[1]
            send_r[k, 4 * NQ + at] = rows[RB - 1]

    sub8 = lax.broadcasted_iota(jnp.int32, (FB, NY), 0)

    def by_freq(table, b):
        values = jnp.zeros((FB, NY), jnp.float32)
        for j in range(FB):
            values = jnp.where(sub8 == j, table[b * FB + j], values)
        return values

    def source(b, carry):
        coup_load(b).wait()
        rows = pl.ds(pl.multiple_of(b * rows_b, rows_b), rows_b)
        product = jnp.dot(coup_v[rows, :], spec_b[...], preferred_element_type=jnp.float32)
        for r in range(RB):
            nonlin[r] = product[:, lanes(r)]
        grow = by_freq(growth, b)
        damp = by_freq(dissipation, b)
        damps = [damp * ratio_v[:, lanes(r)] for r in range(RB)]

        def directions(i, inner):
            for q in range(4):
                d = q * NQ + i
                cosine = trig[d]
                sine = trig[ND + d]
                made = []
                for r in range(RB):
                    forcing = jnp.maximum(cosine * wind_v[0, :, lanes(r)] + sine * wind_v[1, :, lanes(r)], 0.0)
                    value = spec_v[r, pl.ds(b * rows_b + d, FB, stride=ND), :]
                    extra = nonlin[r, pl.ds(d, FB, stride=ND), :]
                    value = value + (grow * (forcing * forcing) - damps[r]) * value + 0.25 * extra
                    energy[b, d, r] = value
                    made.append(value)
                pack(q, i, b, made)
            return inner

        lax.fori_loop(0, NQ, directions, 0)
        to_left(b).start()
        to_right(b).start()
        return carry

    lax.fori_loop(0, blocks, source, 0)

    lane8 = lax.broadcasted_iota(jnp.int32, (FB, NY), 1)
    first_lane = lane8 == 0
    last_lane = lane8 == NY - 1

    def passes(k, b, emit):
        to_left(k).wait_recv()
        to_right(k).wait_recv()
        freqs = pl.ds(pl.multiple_of(b * FB, FB), FB)

        def along_x_and_y(i, carry):
            for q in range(4):
                d = q * NQ + i
                cosine = trig[d]
                sine = trig[ND + d]
                own = [energy[b, d, r] for r in range(RB)]
                at = i + (0 if q in (0, 1) else NQ)
                if q in (0, 3):
                    ext = [recv_l[k, 2 * at] * edge_l, recv_l[k, 2 * at + 1] * edge_l]
                    ext = ext + own + [recv_r[k, 4 * NQ + at] * edge_r]
                    shift = 1
                else:
                    ext = [recv_l[k, 4 * NQ + at] * edge_l] + own
                    ext = ext + [recv_r[k, 2 * at] * edge_r, recv_r[k, 2 * at + 1] * edge_r]
                    shift = 0
                diff = [ext[j + 1] - ext[j] for j in range(RB + 2)]
                second = [diff[j + 1] - diff[j] for j in range(RB + 1)]
                faces = []
                for j in range(RB + 1):
                    nu = cosine * gx[j, freqs, :]
                    faces.append(face_of(nu, ext[j + shift], diff[j + shift], second[j]))
                for r in range(RB):
                    value = own[r] - (faces[r + 1] - faces[r])
                    nu = sine * gy[r, freqs, :]
                    if q in (0, 1):
                        behind = value - jnp.where(first_lane, 0.0, pltpu.roll(value, 1, 1))
                        ahead = pltpu.roll(behind, NY - 1, 1)
                        face = face_of(nu, value, ahead, ahead - behind)
                    else:
                        ahead = jnp.where(last_lane, 0.0, pltpu.roll(value, NY - 1, 1)) - value
                        further = pltpu.roll(ahead, NY - 1, 1)
                        face = face_of(nu, value, ahead, further - ahead)
                    work[d + 1, r] = value - (face - pltpu.roll(face, 1, 1))
            return carry

        lax.fori_loop(0, NQ, along_x_and_y, 0)
        for r in range(RB):
            work[0, r] = work[ND, r]
            work[ND + 1, r] = work[1, r]
            work[ND + 2, r] = work[2, r]

        def turn_face(d, r, base, diff, second, second_next):
            nu = trig[3 * ND + d] * rx[r, freqs, :] - trig[2 * ND + d] * ry[r, freqs, :]
            return face_of(nu, base, diff, jnp.where(nu >= 0.0, second, second_next))

        carry = []
        for r in range(RB):
            e34, e35, e0, e1 = work[ND - 1, r], work[ND, r], work[1, r], work[2, r]
            d34, d35, d0 = e35 - e34, e0 - e35, e1 - e0
            face = turn_face(ND - 1, r, e35, d35, d35 - d34, d0 - d35)
            carry.append((e0, e1, d0, d0 - d35, face))
        carry = tuple(carry)
        for q in range(4):

            def along_directions(i, state, q=q):
                d = q * NQ + i
                made = []
                later = []
                for r in range(RB):
                    e0, e1, diff, second, face_before = state[r]
                    e2 = work[d + 3, r]
                    diff_next = e2 - e1
                    second_next = diff_next - diff
                    face = turn_face(d, r, e0, diff, second, second_next)
                    made.append((e0 - (face - face_before)) * mask_v[r])
                    later.append((e1, e2, diff_next, second_next, face))
                emit(q, i, d, made)
                return tuple(later)

            carry = lax.fori_loop(0, NQ, along_directions, carry)

    def middle(k, carry):
        b = lax.rem(k, blocks)

        def emit(q, i, d, rows):
            for r in range(RB):
                energy[b, d, r] = rows[r]
            pack(q, i, k + blocks, rows)

        passes(k, b, emit)
        to_left(k + blocks).start()
        to_right(k + blocks).start()
        return carry

    lax.fori_loop(0, (SUBSTEPS - 1) * blocks, middle, 0)

    def store(b, r):
        rows = pl.ds(pl.multiple_of(b * rows_b, rows_b), rows_b)
        return pltpu.make_async_copy(out_v.at[r, rows], out.at[rows, lanes(r)], store_sem.at[b, r])

    def final(b, carry):
        def emit(q, i, d, rows):
            for r in range(RB):
                out_v[r, pl.ds(b * rows_b + d, FB, stride=ND), :] = rows[r]

        passes(b + (SUBSTEPS - 1) * blocks, b, emit)
        for r in range(RB):
            store(b, r).start()
        return carry

    lax.fori_loop(0, blocks, final, 0)

    def drain(k, carry):
        to_left(k).wait_send()
        to_right(k).wait_send()
        return carry

    lax.fori_loop(0, SUBSTEPS * blocks, drain, 0)
    for b in range(blocks):
        for r in range(RB):
            store(b, r).wait()


def per_device(
    ncomp,
    nspace,
    spectrum,
    wind_field,
    coupling,
    growth,
    dissipation,
    group_speed,
    refraction,
    depths,
    sea_mask,
    depth_index,
):
    nfreq = growth.shape[0]
    blocks = nfreq // FB
    messages = SUBSTEPS * blocks
    components, points = spectrum.shape
    f32 = jnp.float32
    smem = pl.BlockSpec(memory_space=pltpu.SMEM)
    vmem = pl.BlockSpec(memory_space=pltpu.VMEM)
    hbm = pl.BlockSpec(memory_space=pl.ANY)
    dma = pltpu.SemaphoreType.DMA
    return pl.pallas_call(
        functools.partial(kernel, nfreq, ncomp, nspace),
        out_shape=jax.ShapeDtypeStruct((components, points), f32),
        in_specs=[smem] * 4 + [vmem] * 5 + [hbm] * 2,
        out_specs=hbm,
        scratch_shapes=[
            pltpu.VMEM((RB, components, NY), f32),
            pltpu.VMEM((components, components), jnp.bfloat16),
            pltpu.VMEM((components, points), jnp.bfloat16),
            pltpu.VMEM((RB, FB * ND, NY), f32),
            pltpu.VMEM((blocks, ND, RB, FB, NY), f32),
            pltpu.VMEM((ND + 3, RB, FB, NY), f32),
            pltpu.VMEM((RB, components, NY), f32),
            pltpu.VMEM((messages, SLOTS, FB, NY), f32),
            pltpu.VMEM((messages, SLOTS, FB, NY), f32),
            pltpu.VMEM((messages, SLOTS, FB, NY), f32),
            pltpu.VMEM((messages, SLOTS, FB, NY), f32),
            pltpu.VMEM((2, 2, 8, NY), jnp.int32),
            pltpu.VMEM((2, 2, 8, NY), jnp.int32),
            pltpu.VMEM((RB + 1, nfreq, NY), f32),
            pltpu.VMEM((RB, nfreq, NY), f32),
            pltpu.VMEM((RB, nfreq, NY), f32),
            pltpu.VMEM((RB, nfreq, NY), f32),
            pltpu.VMEM((RB, 8, NY), f32),
            pltpu.VMEM((2, 8, points), f32),
            pltpu.VMEM((8, points), f32),
            dma((RB,)),
            dma((blocks,)),
            dma((blocks, RB)),
            dma((messages,)),
            dma((messages,)),
            dma((messages,)),
            dma((messages,)),
            dma((2,)),
            dma((2,)),
        ],
        compiler_params=pltpu.CompilerParams(
            collective_id=0, has_side_effects=True, vmem_limit_bytes=48 * 1024 * 1024
        ),
    )(
        jnp.asarray(direction_tables()),
        growth,
        dissipation,
        depths,
        wind_field,
        group_speed,
        refraction,
        sea_mask,
        depth_index,
        spectrum,
        coupling,
    )


def solution(mesh):
    in_specs = (
        P(None, ("comp", "space")),
        P(None, ("comp", "space")),
        P(),
        P(),
        P(),
        P(),
        P(),
        P(),
        P("space", None),
        P("space", None),
    )
    out_specs = P(None, ("comp", "space"))
    body = functools.partial(per_device, mesh.shape["comp"], mesh.shape["space"])
    return jax.shard_map(body, mesh=mesh, in_specs=in_specs, out_specs=out_specs, check_vma=False)
```

```python
import functools

import jax
import jax.numpy as jnp
import numpy as np
from jax import lax
from jax.experimental import pallas as pl
from jax.experimental.pallas import tpu as pltpu
from jax.sharding import PartitionSpec as P

ND = 36
NQ = 9
RB = 4
NY = 128
SUBSTEPS = 3
FB = 8
SLOTS = 6 * NQ
MESH = pl.DeviceIdType.MESH


def direction_tables():
    angles = np.float32(2.0 * np.pi) * np.arange(ND, dtype=np.float32) / np.float32(ND)
    cosine = np.cos(angles.astype(np.float64)).astype(np.float32)
    sine = np.sin(angles.astype(np.float64)).astype(np.float32)
    half_cos = np.float32(0.5) * (cosine + np.roll(cosine, -1))
    half_sin = np.float32(0.5) * (sine + np.roll(sine, -1))
    return np.concatenate([cosine, sine, half_cos, half_sin])


def face_of(nu, base, diff, second):
    return nu * (base + (1.0 - nu) * (0.5 * diff - (nu * (1.0 / 6.0) + (1.0 / 6.0)) * second))


def kernel(
    nfreq,
    ncomp,
    nspace,
    spectrum,
    wind_hbm,
    coupling,
    growth_hbm,
    dissipation_hbm,
    group_speed_hbm,
    refraction_hbm,
    depths_hbm,
    sea_mask_hbm,
    depth_index_hbm,
    out,
    trig,
    growth,
    dissipation,
    depths,
    wind,
    group_speed,
    refraction,
    sea_mask,
    depth_index,
    spec_v,
    coup_v,
    spec_b,
    nonlin,
    energy,
    work,
    out_v,
    send_l,
    send_r,
    recv_l,
    recv_r,
    coast_out,
    coast_in,
    gx,
    gy,
    rx,
    ry,
    mask_v,
    wind_v,
    ratio_v,
    small_sem,
    load_sem,
    coup_sem,
    store_sem,
    send_l_sem,
    send_r_sem,
    recv_l_sem,
    recv_r_sem,
    coast_send_sem,
    coast_recv_sem,
):
    blocks = nfreq // FB
    rows_b = FB * ND
    components = nfreq * ND
    c = lax.axis_index("comp")
    s = lax.axis_index("space")
    total = ncomp * nspace
    n = s * ncomp + c
    before = lax.rem(n + total - 1, total)
    after = lax.rem(n + 1, total)
    left = (lax.rem(before, ncomp), lax.div(before, ncomp))
    right = (lax.rem(after, ncomp), lax.div(after, ncomp))
    edge_l = jnp.where(n > 0, 1.0, 0.0).astype(jnp.float32)
    edge_r = jnp.where(n < total - 1, 1.0, 0.0).astype(jnp.float32)

    barrier = pltpu.get_barrier_semaphore()
    pl.semaphore_signal(barrier, inc=1, device_id=left, device_id_type=MESH)
    pl.semaphore_signal(barrier, inc=1, device_id=right, device_id_type=MESH)

    def lanes(r):
        return slice(r * NY, (r + 1) * NY)

    def spec_load(r):
        return pltpu.make_async_copy(spectrum.at[:, lanes(r)], spec_v.at[r], load_sem.at[r])

    for r in range(RB):
        spec_load(r).start()
    own_tile = pl.ds(pl.multiple_of(lax.div(c * RB, 8) * 8, 8), 8)
    small_loads = [
        pltpu.make_async_copy(src, dst, small_sem.at[j])
        for j, (src, dst) in enumerate(
            (
                (sea_mask_hbm.at[own_tile], sea_mask),
                (depth_index_hbm.at[own_tile], depth_index),
                (wind_hbm, wind),
                (growth_hbm, growth),
                (dissipation_hbm, dissipation),
                (group_speed_hbm, group_speed),
                (refraction_hbm, refraction),
                (depths_hbm, depths),
            )
        )
    ]
    for load in small_loads:
        load.start()

    def coup_load(b):
        rows = pl.ds(pl.multiple_of(b * rows_b, rows_b), rows_b)
        return pltpu.make_async_copy(coupling.at[rows], coup_v.at[rows], coup_sem.at[b])

    for b in range(blocks):
        coup_load(b).start()

    for at, value in enumerate(direction_tables()):
        trig[at] = jnp.float32(value)
    for load in small_loads:
        load.wait()

    def to_left(k):
        return pltpu.make_async_remote_copy(
            src_ref=send_l.at[k],
            dst_ref=recv_r.at[k],
            send_sem=send_l_sem.at[k],
            recv_sem=recv_r_sem.at[k],
            device_id=left,
            device_id_type=MESH,
        )

    def to_right(k):
        return pltpu.make_async_remote_copy(
            src_ref=send_r.at[k],
            dst_ref=recv_l.at[k],
            send_sem=send_r_sem.at[k],
            recv_sem=recv_l_sem.at[k],
            device_id=right,
            device_id_type=MESH,
        )

    for r in range(RB):
        spec_load(r).wait()

        def cast_rows(i, acc, r=r):
            rows = pl.ds(pl.multiple_of(i * 64, 64), 64)
            block = spec_v[r, rows, :]
            spec_b[rows, lanes(r)] = block.astype(jnp.bfloat16)
            return acc + jnp.sum(block.reshape(8, 8, NY), axis=0)

        acc = lax.fori_loop(0, components // 64, cast_rows, jnp.zeros((8, NY), jnp.float32))
        average = jnp.sum(acc, axis=0, keepdims=True) * (1.0 / components)
        ratio_v[:, lanes(r)] = jnp.broadcast_to(average / (average + 1.0), (8, NY))
    wind_v[0] = jnp.broadcast_to(wind[0:1, :], (8, RB * NY))
    wind_v[1] = jnp.broadcast_to(wind[1:2, :], (8, RB * NY))

    def pack(q, i, k, rows):
        if q in (0, 3):
            at = i + (0 if q == 0 else NQ)
            send_r[k, 2 * at] = rows[RB - 2]
            send_r[k, 2 * at + 1] = rows[RB - 1]
            send_l[k, 4 * NQ + at] = rows[0]
        else:
            at = i + (0 if q == 1 else NQ)
            send_l[k, 2 * at] = rows[0]
            send_l[k, 2 * at + 1] = rows[1]
            send_r[k, 4 * NQ + at] = rows[RB - 1]

    sub8 = lax.broadcasted_iota(jnp.int32, (FB, NY), 0)

    def by_freq(table, b):
        values = jnp.zeros((FB, NY), jnp.float32)
        for j in range(FB):
            values = jnp.where(sub8 == j, table[b * FB + j], values)
        return values

    def source(b):
        coup_load(b).wait()
        rows = pl.ds(pl.multiple_of(b * rows_b, rows_b), rows_b)
        product = jnp.dot(coup_v[rows, :], spec_b[...], preferred_element_type=jnp.float32)
        for r in range(RB):
            nonlin[r] = product[:, lanes(r)]
        grow = by_freq(growth, b)
        damp = by_freq(dissipation, b)
        damps = [damp * ratio_v[:, lanes(r)] for r in range(RB)]

        def directions(i, inner):
            for q in range(4):
                d = q * NQ + i
                cosine = trig[d]
                sine = trig[ND + d]
                made = []
                for r in range(RB):
                    forcing = jnp.maximum(cosine * wind_v[0, :, lanes(r)] + sine * wind_v[1, :, lanes(r)], 0.0)
                    value = spec_v[r, pl.ds(b * rows_b + d, FB, stride=ND), :]
                    extra = nonlin[r, pl.ds(d, FB, stride=ND), :]
                    value = value + (grow * (forcing * forcing) - damps[r]) * value + 0.25 * extra
                    energy[b, d, r] = value
                    made.append(value)
                pack(q, i, b, made)
            return inner

        lax.fori_loop(0, NQ, directions, 0, unroll=3)

    def source_and_send(b, carry):
        source(b)
        to_left(b).start()
        to_right(b).start()
        return carry

    source(0)

    row0 = lax.rem(c * RB, 8)
    own_mask = [sea_mask[pl.ds(row0 + r, 1), :] for r in range(RB)]
    own_index = [depth_index[pl.ds(row0 + r, 1), :] for r in range(RB)]
    for side, r in ((0, 0), (1, RB - 1)):
        coast_out[side, 0] = jnp.broadcast_to(own_mask[r], (8, NY))
        coast_out[side, 1] = jnp.broadcast_to(own_index[r], (8, NY))

    pl.semaphore_wait(barrier, 2)

    def coast_copy(side):
        return pltpu.make_async_remote_copy(
            src_ref=coast_out.at[side],
            dst_ref=coast_in.at[1 - side],
            send_sem=coast_send_sem.at[side],
            recv_sem=coast_recv_sem.at[1 - side],
            device_id=left if side == 0 else right,
            device_id_type=MESH,
        )

    for side in range(2):
        coast_copy(side).start()

    to_left(0).start()
    to_right(0).start()
    lax.fori_loop(1, blocks, source_and_send, 0)

    for side in range(2):
        coast_copy(side).wait()
    mask_rows = (
        [coast_in[0, 0, 0:1, :].astype(jnp.float32) * edge_l]
        + [m.astype(jnp.float32) for m in own_mask]
        + [coast_in[1, 0, 0:1, :].astype(jnp.float32) * edge_r]
    )
    index_rows = [coast_in[0, 1, 0:1, :]] + own_index + [coast_in[1, 1, 0:1, :]]
    levels = depths.shape[0]
    level = lax.broadcasted_iota(jnp.int32, (levels, NY), 0)
    onehot = jnp.concatenate(
        [(jnp.broadcast_to(row, (levels, NY)) == level).astype(jnp.float32) for row in index_rows], axis=1
    )
    speeds = jnp.dot(
        group_speed[...], onehot, precision=lax.Precision.HIGHEST, preferred_element_type=jnp.float32
    )
    turning = jnp.dot(
        refraction[...],
        onehot[:, NY : (RB + 1) * NY],
        precision=lax.Precision.HIGHEST,
        preferred_element_type=jnp.float32,
    )
    lane_row = lax.broadcasted_iota(jnp.int32, (1, NY), 1)
    heights = []
    for row, mask in zip(index_rows, mask_rows):
        height = jnp.zeros((1, NY), jnp.float32)
        for entry in range(levels):
            height = jnp.where(row == entry, depths[entry], height)
        heights.append(height * mask)
    for j in range(RB + 1):
        pair = 0.5 * (speeds[:, lanes(j)] + speeds[:, lanes(j + 1)])
        gx[j] = pair * (mask_rows[j] * mask_rows[j + 1])
    for r in range(RB):
        mask = mask_rows[r + 1]
        own = speeds[:, lanes(r + 1)]
        beyond = jnp.where(lane_row == NY - 1, 0.0, pltpu.roll(jnp.broadcast_to(mask, (8, NY)), NY - 1, 1)[:1])
        gy[r] = 0.5 * (own + pltpu.roll(own, NY - 1, 1)) * (mask * beyond)
        wide = jnp.broadcast_to(heights[r + 1], (8, NY))
        up = jnp.where(lane_row == NY - 1, 0.0, pltpu.roll(wide, NY - 1, 1)[:1])
        down = jnp.where(lane_row == 0, 0.0, pltpu.roll(wide, 1, 1)[:1])
        rx[r] = turning[:, lanes(r)] * (0.5 * (heights[r + 2] - heights[r]))
        ry[r] = turning[:, lanes(r)] * (0.5 * (up - down))
        mask_v[r] = jnp.broadcast_to(mask, (8, NY))


    lane8 = lax.broadcasted_iota(jnp.int32, (FB, NY), 1)
    first_lane = lane8 == 0
    last_lanes = lane8 >= NY - 2

    def passes(k, b, emit):
        to_left(k).wait_recv()
        to_right(k).wait_recv()
        freqs = pl.ds(pl.multiple_of(b * FB, FB), FB)

        def along_x_and_y(i, carry):
            for q in range(4):
                d = q * NQ + i
                cosine = trig[d]
                sine = trig[ND + d]
                own = [energy[b, d, r] for r in range(RB)]
                at = i + (0 if q in (0, 1) else NQ)
                if q in (0, 3):
                    ext = [recv_l[k, 2 * at] * edge_l, recv_l[k, 2 * at + 1] * edge_l]
                    ext = ext + own + [recv_r[k, 4 * NQ + at] * edge_r]
                    shift = 1
                else:
                    ext = [recv_l[k, 4 * NQ + at] * edge_l] + own
                    ext = ext + [recv_r[k, 2 * at] * edge_r, recv_r[k, 2 * at + 1] * edge_r]
                    shift = 0
                diff = [ext[j + 1] - ext[j] for j in range(RB + 2)]
                second = [diff[j + 1] - diff[j] for j in range(RB + 1)]
                faces = []
                for j in range(RB + 1):
                    nu = cosine * gx[j, freqs, :]
                    faces.append(face_of(nu, ext[j + shift], diff[j + shift], second[j]))
                for r in range(RB):
                    value = own[r] - (faces[r + 1] - faces[r])
                    nu = sine * gy[r, freqs, :]
                    if q in (0, 1):
                        behind = value - jnp.where(first_lane, 0.0, pltpu.roll(value, 1, 1))
                        ahead = pltpu.roll(value, NY - 1, 1) - value
                        face = face_of(nu, value, ahead, ahead - behind)
                    else:
                        next1 = pltpu.roll(value, NY - 1, 1)
                        next2 = jnp.where(last_lanes, 0.0, pltpu.roll(value, NY - 2, 1))
                        ahead = next1 - value
                        face = face_of(nu, value, ahead, next2 - next1 - ahead)
                    work[d + 1, r] = value - (face - pltpu.roll(face, 1, 1))
            return carry

        lax.fori_loop(0, NQ, along_x_and_y, 0, unroll=3)
        for r in range(RB):
            work[0, r] = work[ND, r]
            work[ND + 1, r] = work[1, r]
            work[ND + 2, r] = work[2, r]

        def turn_face(d, r, base, diff, second, second_next):
            nu = trig[3 * ND + d] * rx[r, freqs, :] - trig[2 * ND + d] * ry[r, freqs, :]
            return face_of(nu, base, diff, jnp.where(nu >= 0.0, second, second_next))

        carry = []
        for r in range(RB):
            e34, e35, e0, e1 = work[ND - 1, r], work[ND, r], work[1, r], work[2, r]
            d34, d35, d0 = e35 - e34, e0 - e35, e1 - e0
            face = turn_face(ND - 1, r, e35, d35, d35 - d34, d0 - d35)
            carry.append((e0, e1, d0, d0 - d35, face))
        carry = tuple(carry)
        for q in range(4):

            def along_directions(i, state, q=q):
                d = q * NQ + i
                made = []
                later = []
                for r in range(RB):
                    e0, e1, diff, second, face_before = state[r]
                    e2 = work[d + 3, r]
                    diff_next = e2 - e1
                    second_next = diff_next - diff
                    face = turn_face(d, r, e0, diff, second, second_next)
                    made.append((e0 - (face - face_before)) * mask_v[r])
                    later.append((e1, e2, diff_next, second_next, face))
                emit(q, i, d, made)
                return tuple(later)

            carry = lax.fori_loop(0, NQ, along_directions, carry, unroll=3)

    def middle(k, carry):
        b = lax.rem(k, blocks)

        def emit(q, i, d, rows):
            for r in range(RB):
                energy[b, d, r] = rows[r]
            pack(q, i, k + blocks, rows)

        passes(k, b, emit)
        to_left(k + blocks).start()
        to_right(k + blocks).start()
        return carry

    lax.fori_loop(0, (SUBSTEPS - 1) * blocks, middle, 0)

    def store(b, r):
        rows = pl.ds(pl.multiple_of(b * rows_b, rows_b), rows_b)
        return pltpu.make_async_copy(out_v.at[r, rows], out.at[rows, lanes(r)], store_sem.at[b, r])

    def final(b, carry):
        def emit(q, i, d, rows):
            for r in range(RB):
                out_v[r, pl.ds(b * rows_b + d, FB, stride=ND), :] = rows[r]

        passes(b + (SUBSTEPS - 1) * blocks, b, emit)
        for r in range(RB):
            store(b, r).start()
        return carry

    lax.fori_loop(0, blocks, final, 0)

    def drain(k, carry):
        to_left(k).wait_send()
        to_right(k).wait_send()
        return carry

    lax.fori_loop(0, SUBSTEPS * blocks, drain, 0)
    for b in range(blocks):
        for r in range(RB):
            store(b, r).wait()


def hand_on(moved, out, load_sems, store_sems, buf):
    chunks = load_sems.shape[0]
    rows = moved.shape[0] // chunks
    at = [pl.ds(j * rows, rows) for j in range(chunks)]
    loads = [pltpu.make_async_copy(moved.at[at[j]], buf.at[at[j]], load_sems.at[j]) for j in range(chunks)]
    stores = [pltpu.make_async_copy(buf.at[at[j]], out.at[at[j]], store_sems.at[j]) for j in range(chunks)]
    for copy in loads:
        copy.start()
    for load, copy in zip(loads, stores):
        load.wait()
        copy.start()
    for copy in stores:
        copy.wait()


def per_device(
    ncomp,
    nspace,
    spectrum,
    wind_field,
    coupling,
    growth,
    dissipation,
    group_speed,
    refraction,
    depths,
    sea_mask,
    depth_index,
):
    nfreq = growth.shape[0]
    blocks = nfreq // FB
    messages = SUBSTEPS * blocks
    components, points = spectrum.shape
    f32 = jnp.float32
    hbm = pl.BlockSpec(memory_space=pl.ANY)
    dma = pltpu.SemaphoreType.DMA
    moved = pl.pallas_call(
        functools.partial(kernel, nfreq, ncomp, nspace),
        out_shape=jax.ShapeDtypeStruct((components, points), f32),
        in_specs=[hbm] * 10,
        out_specs=hbm,
        scratch_shapes=[
            pltpu.SMEM((4 * ND,), f32),
            pltpu.SMEM(growth.shape, f32),
            pltpu.SMEM(dissipation.shape, f32),
            pltpu.SMEM(depths.shape, f32),
            pltpu.VMEM(wind_field.shape, f32),
            pltpu.VMEM(group_speed.shape, f32),
            pltpu.VMEM(refraction.shape, f32),
            pltpu.VMEM((8, NY), jnp.int32),
            pltpu.VMEM((8, NY), jnp.int32),
            pltpu.VMEM((RB, components, NY), f32),
            pltpu.VMEM((components, components), jnp.bfloat16),
            pltpu.VMEM((components, points), jnp.bfloat16),
            pltpu.VMEM((RB, FB * ND, NY), f32),
            pltpu.VMEM((blocks, ND, RB, FB, NY), f32),
            pltpu.VMEM((ND + 3, RB, FB, NY), f32),
            pltpu.VMEM((RB, components, NY), f32),
            pltpu.VMEM((messages, SLOTS, FB, NY), f32),
            pltpu.VMEM((messages, SLOTS, FB, NY), f32),
            pltpu.VMEM((messages, SLOTS, FB, NY), f32),
            pltpu.VMEM((messages, SLOTS, FB, NY), f32),
            pltpu.VMEM((2, 2, 8, NY), jnp.int32),
            pltpu.VMEM((2, 2, 8, NY), jnp.int32),
            pltpu.VMEM((RB + 1, nfreq, NY), f32),
            pltpu.VMEM((RB, nfreq, NY), f32),
            pltpu.VMEM((RB, nfreq, NY), f32),
            pltpu.VMEM((RB, nfreq, NY), f32),
            pltpu.VMEM((RB, 8, NY), f32),
            pltpu.VMEM((2, 8, points), f32),
            pltpu.VMEM((8, points), f32),
            dma((8,)),
            dma((RB,)),
            dma((blocks,)),
            dma((blocks, RB)),
            dma((messages,)),
            dma((messages,)),
            dma((messages,)),
            dma((messages,)),
            dma((2,)),
            dma((2,)),
        ],
        compiler_params=pltpu.CompilerParams(
            collective_id=0, has_side_effects=True, vmem_limit_bytes=64 * 1024 * 1024 - 4096
        ),
    )(
        spectrum,
        wind_field,
        coupling,
        growth,
        dissipation,
        group_speed,
        refraction,
        depths,
        sea_mask,
        depth_index,
    )
    chunks = 8
    return pl.pallas_call(
        hand_on,
        out_shape=jax.ShapeDtypeStruct((components, points), f32),
        in_specs=[hbm],
        out_specs=hbm,
        scratch_shapes=[dma((chunks,)), dma((chunks,)), pltpu.VMEM((components, points), f32)],
    )(moved)


def solution(mesh):
    in_specs = (
        P(None, ("comp", "space")),
        P(None, ("comp", "space")),
        P(),
        P(),
        P(),
        P(),
        P(),
        P(),
        P("space", None),
        P("space", None),
    )
    out_specs = P(None, ("comp", "space"))
    body = functools.partial(per_device, mesh.shape["comp"], mesh.shape["space"])
    return jax.shard_map(body, mesh=mesh, in_specs=in_specs, out_specs=out_specs, check_vma=False)
```

```python
import functools

import jax
import jax.numpy as jnp
import numpy as np
from jax import lax
from jax.experimental import pallas as pl
from jax.experimental.pallas import tpu as pltpu
from jax.sharding import PartitionSpec as P

ND = 36
NQ = 9
RB = 4
NY = 128
SUBSTEPS = 3
FB = 8
SLOTS = 6 * NQ
PAIRS = ((2, 3), (0, 1))
MESH = pl.DeviceIdType.MESH


def direction_tables():
    angles = np.float32(2.0 * np.pi) * np.arange(ND, dtype=np.float32) / np.float32(ND)
    cosine = np.cos(angles.astype(np.float64)).astype(np.float32)
    sine = np.sin(angles.astype(np.float64)).astype(np.float32)
    half_cos = np.float32(0.5) * (cosine + np.roll(cosine, -1))
    half_sin = np.float32(0.5) * (sine + np.roll(sine, -1))
    return np.concatenate([cosine, sine, half_cos, half_sin])


def face_of(nu, base, diff, second):
    return nu * (base + (1.0 - nu) * (0.5 * diff - (nu * (1.0 / 6.0) + (1.0 / 6.0)) * second))


def kernel(
    nfreq,
    ncomp,
    nspace,
    spectrum,
    wind_hbm,
    coupling,
    growth_hbm,
    dissipation_hbm,
    group_speed_hbm,
    refraction_hbm,
    depths_hbm,
    sea_mask_hbm,
    depth_index_hbm,
    out,
    trig,
    growth,
    dissipation,
    depths,
    wind,
    group_speed,
    refraction,
    sea_mask,
    depth_index,
    spec_v,
    coup_v,
    spec_b,
    nonlin,
    energy,
    work,
    out_v,
    send_l,
    send_r,
    recv_l,
    recv_r,
    coast_out,
    coast_in,
    gx,
    gy,
    rx,
    ry,
    mask_v,
    wind_v,
    ratio_v,
    small_sem,
    load_sem,
    coup_sem,
    store_sem,
    send_l_sem,
    send_r_sem,
    recv_l_sem,
    recv_r_sem,
    coast_send_sem,
    coast_recv_sem,
):
    blocks = nfreq // FB
    rows_b = FB * ND
    components = nfreq * ND
    c = lax.axis_index("comp")
    s = lax.axis_index("space")
    total = ncomp * nspace
    n = s * ncomp + c
    before = lax.rem(n + total - 1, total)
    after = lax.rem(n + 1, total)
    left = (lax.rem(before, ncomp), lax.div(before, ncomp))
    right = (lax.rem(after, ncomp), lax.div(after, ncomp))
    edge_l = jnp.where(n > 0, 1.0, 0.0).astype(jnp.float32)
    edge_r = jnp.where(n < total - 1, 1.0, 0.0).astype(jnp.float32)

    barrier = pltpu.get_barrier_semaphore()
    pl.semaphore_signal(barrier, inc=1, device_id=left, device_id_type=MESH)
    pl.semaphore_signal(barrier, inc=1, device_id=right, device_id_type=MESH)

    def lanes(r):
        return slice(r * NY, (r + 1) * NY)

    def spec_load(r):
        return pltpu.make_async_copy(spectrum.at[:, lanes(r)], spec_v.at[r], load_sem.at[r])

    own_tile = pl.ds(pl.multiple_of(lax.div(c * RB, 8) * 8, 8), 8)
    small_loads = [
        pltpu.make_async_copy(src, dst, small_sem.at[j])
        for j, (src, dst) in enumerate(
            (
                (sea_mask_hbm.at[own_tile], sea_mask),
                (depth_index_hbm.at[own_tile], depth_index),
                (wind_hbm, wind),
                (growth_hbm, growth),
                (dissipation_hbm, dissipation),
                (group_speed_hbm, group_speed),
                (refraction_hbm, refraction),
                (depths_hbm, depths),
            )
        )
    ]
    for load in small_loads:
        load.start()

    def coup_load(b):
        rows = pl.ds(pl.multiple_of(b * rows_b, rows_b), rows_b)
        return pltpu.make_async_copy(coupling.at[rows], coup_v.at[rows], coup_sem.at[b])

    coup_load(0).start()
    for r in PAIRS[0]:
        spec_load(r).start()

    for at, value in enumerate(direction_tables()):
        trig[at] = jnp.float32(value)
    for load in small_loads:
        load.wait()

    def to_left(k):
        return pltpu.make_async_remote_copy(
            src_ref=send_l.at[k],
            dst_ref=recv_r.at[k],
            send_sem=send_l_sem.at[k],
            recv_sem=recv_r_sem.at[k],
            device_id=left,
            device_id_type=MESH,
        )

    def to_right(k):
        return pltpu.make_async_remote_copy(
            src_ref=send_r.at[k],
            dst_ref=recv_l.at[k],
            send_sem=send_r_sem.at[k],
            recv_sem=recv_l_sem.at[k],
            device_id=right,
            device_id_type=MESH,
        )

    wind_v[0] = jnp.broadcast_to(wind[0:1, :], (8, RB * NY))
    wind_v[1] = jnp.broadcast_to(wind[1:2, :], (8, RB * NY))

    def pack_right(q, i, k, rows):
        at = i + (0 if q in (0, 1) else NQ)
        if q in (0, 3):
            send_r[k, 2 * at] = rows[RB - 2]
            send_r[k, 2 * at + 1] = rows[RB - 1]
        else:
            send_r[k, 4 * NQ + at] = rows[RB - 1]

    def pack_left(q, i, k, rows):
        at = i + (0 if q in (0, 1) else NQ)
        if q in (0, 3):
            send_l[k, 4 * NQ + at] = rows[0]
        else:
            send_l[k, 2 * at] = rows[0]
            send_l[k, 2 * at + 1] = rows[1]

    sub8 = lax.broadcasted_iota(jnp.int32, (FB, NY), 0)

    def by_freq(table, b):
        values = jnp.zeros((FB, NY), jnp.float32)
        for j in range(FB):
            values = jnp.where(sub8 == j, table[b * FB + j], values)
        return values

    def prepare(r):
        spec_load(r).wait()

        def cast_rows(i, acc):
            rows = pl.ds(pl.multiple_of(i * 64, 64), 64)
            block = spec_v[r, rows, :]
            spec_b[rows, lanes(r)] = block.astype(jnp.bfloat16)
            return acc + jnp.sum(block.reshape(8, 8, NY), axis=0)

        acc = lax.fori_loop(0, components // 64, cast_rows, jnp.zeros((8, NY), jnp.float32))
        average = jnp.sum(acc, axis=0, keepdims=True) * (1.0 / components)
        ratio_v[:, lanes(r)] = jnp.broadcast_to(average / (average + 1.0), (8, NY))

    def source(b, pair):
        rows = pl.ds(pl.multiple_of(b * rows_b, rows_b), rows_b)
        columns = slice(pair[0] * NY, (pair[-1] + 1) * NY)
        product = jnp.dot(coup_v[rows, :], spec_b[:, columns], preferred_element_type=jnp.float32)
        for at, r in enumerate(pair):
            nonlin[r] = product[:, lanes(at)]
        grow = by_freq(growth, b)
        damp = by_freq(dissipation, b)
        damps = {r: damp * ratio_v[:, lanes(r)] for r in pair}

        def directions(i, inner):
            for q in range(4):
                d = q * NQ + i
                cosine = trig[d]
                sine = trig[ND + d]
                made = {}
                for r in pair:
                    forcing = jnp.maximum(cosine * wind_v[0, :, lanes(r)] + sine * wind_v[1, :, lanes(r)], 0.0)
                    value = spec_v[r, pl.ds(b * rows_b + d, FB, stride=ND), :]
                    extra = nonlin[r, pl.ds(d, FB, stride=ND), :]
                    value = value + (grow * (forcing * forcing) - damps[r]) * value + 0.25 * extra
                    energy[b, d, r] = value
                    made[r] = value
                if pair == PAIRS[0]:
                    pack_right(q, i, b, made)
                else:
                    pack_left(q, i, b, made)
            return inner

        lax.fori_loop(0, NQ, directions, 0, unroll=3)

    def source_and_send(b, carry):
        coup_load(b).wait()
        source(b, PAIRS[0])
        to_right(b).start()
        source(b, PAIRS[1])
        to_left(b).start()
        return carry

    prepare(PAIRS[0][0])
    for r in PAIRS[1]:
        spec_load(r).start()
    prepare(PAIRS[0][1])
    coup_load(0).wait()
    source(0, PAIRS[0])

    row0 = lax.rem(c * RB, 8)
    own_mask = [sea_mask[pl.ds(row0 + r, 1), :] for r in range(RB)]
    own_index = [depth_index[pl.ds(row0 + r, 1), :] for r in range(RB)]
    for side, r in ((0, 0), (1, RB - 1)):
        coast_out[side, 0] = jnp.broadcast_to(own_mask[r], (8, NY))
        coast_out[side, 1] = jnp.broadcast_to(own_index[r], (8, NY))

    pl.semaphore_wait(barrier, 2)

    def coast_copy(side):
        return pltpu.make_async_remote_copy(
            src_ref=coast_out.at[side],
            dst_ref=coast_in.at[1 - side],
            send_sem=coast_send_sem.at[side],
            recv_sem=coast_recv_sem.at[1 - side],
            device_id=left if side == 0 else right,
            device_id_type=MESH,
        )

    for side in range(2):
        coast_copy(side).start()

    to_right(0).start()
    for r in PAIRS[1]:
        prepare(r)
    for b in range(1, blocks):
        coup_load(b).start()
    source(0, PAIRS[1])
    to_left(0).start()
    lax.fori_loop(1, blocks, source_and_send, 0)

    for side in range(2):
        coast_copy(side).wait()
    mask_rows = (
        [coast_in[0, 0, 0:1, :].astype(jnp.float32) * edge_l]
        + [m.astype(jnp.float32) for m in own_mask]
        + [coast_in[1, 0, 0:1, :].astype(jnp.float32) * edge_r]
    )
    index_rows = [coast_in[0, 1, 0:1, :]] + own_index + [coast_in[1, 1, 0:1, :]]
    levels = depths.shape[0]
    level = lax.broadcasted_iota(jnp.int32, (levels, NY), 0)
    onehot = jnp.concatenate(
        [(jnp.broadcast_to(row, (levels, NY)) == level).astype(jnp.float32) for row in index_rows], axis=1
    )
    speeds = jnp.dot(
        group_speed[...], onehot, precision=lax.Precision.HIGHEST, preferred_element_type=jnp.float32
    )
    turning = jnp.dot(
        refraction[...],
        onehot[:, NY : (RB + 1) * NY],
        precision=lax.Precision.HIGHEST,
        preferred_element_type=jnp.float32,
    )
    lane_row = lax.broadcasted_iota(jnp.int32, (1, NY), 1)
    heights = []
    for row, mask in zip(index_rows, mask_rows):
        height = jnp.zeros((1, NY), jnp.float32)
        for entry in range(levels):
            height = jnp.where(row == entry, depths[entry], height)
        heights.append(height * mask)
    for j in range(RB + 1):
        pair = 0.5 * (speeds[:, lanes(j)] + speeds[:, lanes(j + 1)])
        gx[j] = pair * (mask_rows[j] * mask_rows[j + 1])
    for r in range(RB):
        mask = mask_rows[r + 1]
        own = speeds[:, lanes(r + 1)]
        beyond = jnp.where(lane_row == NY - 1, 0.0, pltpu.roll(jnp.broadcast_to(mask, (8, NY)), NY - 1, 1)[:1])
        gy[r] = 0.5 * (own + pltpu.roll(own, NY - 1, 1)) * (mask * beyond)
        wide = jnp.broadcast_to(heights[r + 1], (8, NY))
        up = jnp.where(lane_row == NY - 1, 0.0, pltpu.roll(wide, NY - 1, 1)[:1])
        down = jnp.where(lane_row == 0, 0.0, pltpu.roll(wide, 1, 1)[:1])
        rx[r] = turning[:, lanes(r)] * (0.5 * (heights[r + 2] - heights[r]))
        ry[r] = turning[:, lanes(r)] * (0.5 * (up - down))
        mask_v[r] = jnp.broadcast_to(mask, (8, NY))


    lane8 = lax.broadcasted_iota(jnp.int32, (FB, NY), 1)
    first_lane = lane8 == 0
    last_lanes = lane8 >= NY - 2

    def passes(k, b, emit):
        to_left(k).wait_recv()
        to_right(k).wait_recv()
        freqs = pl.ds(pl.multiple_of(b * FB, FB), FB)

        def along_x_and_y(i, carry):
            for q in range(4):
                d = q * NQ + i
                cosine = trig[d]
                sine = trig[ND + d]
                own = [energy[b, d, r] for r in range(RB)]
                at = i + (0 if q in (0, 1) else NQ)
                if q in (0, 3):
                    ext = [recv_l[k, 2 * at] * edge_l, recv_l[k, 2 * at + 1] * edge_l]
                    ext = ext + own + [recv_r[k, 4 * NQ + at] * edge_r]
                    shift = 1
                else:
                    ext = [recv_l[k, 4 * NQ + at] * edge_l] + own
                    ext = ext + [recv_r[k, 2 * at] * edge_r, recv_r[k, 2 * at + 1] * edge_r]
                    shift = 0
                diff = [ext[j + 1] - ext[j] for j in range(RB + 2)]
                second = [diff[j + 1] - diff[j] for j in range(RB + 1)]
                faces = []
                for j in range(RB + 1):
                    nu = cosine * gx[j, freqs, :]
                    faces.append(face_of(nu, ext[j + shift], diff[j + shift], second[j]))
                for r in range(RB):
                    value = own[r] - (faces[r + 1] - faces[r])
                    nu = sine * gy[r, freqs, :]
                    if q in (0, 1):
                        behind = value - jnp.where(first_lane, 0.0, pltpu.roll(value, 1, 1))
                        ahead = pltpu.roll(value, NY - 1, 1) - value
                        face = face_of(nu, value, ahead, ahead - behind)
                    else:
                        next1 = pltpu.roll(value, NY - 1, 1)
                        next2 = jnp.where(last_lanes, 0.0, pltpu.roll(value, NY - 2, 1))
                        ahead = next1 - value
                        face = face_of(nu, value, ahead, next2 - next1 - ahead)
                    work[d + 1, r] = value - (face - pltpu.roll(face, 1, 1))
            return carry

        lax.fori_loop(0, NQ, along_x_and_y, 0, unroll=3)
        for r in range(RB):
            work[0, r] = work[ND, r]
            work[ND + 1, r] = work[1, r]
            work[ND + 2, r] = work[2, r]

        def turn_face(d, r, base, diff, second, second_next):
            nu = trig[3 * ND + d] * rx[r, freqs, :] - trig[2 * ND + d] * ry[r, freqs, :]
            return face_of(nu, base, diff, jnp.where(nu >= 0.0, second, second_next))

        carry = []
        for r in range(RB):
            e34, e35, e0, e1 = work[ND - 1, r], work[ND, r], work[1, r], work[2, r]
            d34, d35, d0 = e35 - e34, e0 - e35, e1 - e0
            face = turn_face(ND - 1, r, e35, d35, d35 - d34, d0 - d35)
            carry.append((e0, e1, d0, d0 - d35, face))
        carry = tuple(carry)
        for q in range(4):

            def along_directions(i, state, q=q):
                d = q * NQ + i
                made = []
                later = []
                for r in range(RB):
                    e0, e1, diff, second, face_before = state[r]
                    e2 = work[d + 3, r]
                    diff_next = e2 - e1
                    second_next = diff_next - diff
                    face = turn_face(d, r, e0, diff, second, second_next)
                    made.append((e0 - (face - face_before)) * mask_v[r])
                    later.append((e1, e2, diff_next, second_next, face))
                emit(q, i, d, made)
                return tuple(later)

            carry = lax.fori_loop(0, NQ, along_directions, carry, unroll=3)

    def middle(k, carry):
        b = lax.rem(k, blocks)

        def emit(q, i, d, rows):
            for r in range(RB):
                energy[b, d, r] = rows[r]
            pack_right(q, i, k + blocks, rows)
            pack_left(q, i, k + blocks, rows)

        passes(k, b, emit)
        to_right(k + blocks).start()
        to_left(k + blocks).start()
        return carry

    lax.fori_loop(0, (SUBSTEPS - 1) * blocks, middle, 0)

    def store(b, r):
        rows = pl.ds(pl.multiple_of(b * rows_b, rows_b), rows_b)
        return pltpu.make_async_copy(out_v.at[r, rows], out.at[rows, lanes(r)], store_sem.at[b, r])

    def final(b, carry):
        def emit(q, i, d, rows):
            for r in range(RB):
                out_v[r, pl.ds(b * rows_b + d, FB, stride=ND), :] = rows[r]

        passes(b + (SUBSTEPS - 1) * blocks, b, emit)
        for r in range(RB):
            store(b, r).start()
        return carry

    lax.fori_loop(0, blocks, final, 0)

    def drain(k, carry):
        to_left(k).wait_send()
        to_right(k).wait_send()
        return carry

    lax.fori_loop(0, SUBSTEPS * blocks, drain, 0)
    for b in range(blocks):
        for r in range(RB):
            store(b, r).wait()


def hand_on(moved, out, load_sems, store_sems, buf):
    chunks = load_sems.shape[0]
    rows = moved.shape[0] // chunks
    at = [pl.ds(j * rows, rows) for j in range(chunks)]
    loads = [pltpu.make_async_copy(moved.at[at[j]], buf.at[at[j]], load_sems.at[j]) for j in range(chunks)]
    stores = [pltpu.make_async_copy(buf.at[at[j]], out.at[at[j]], store_sems.at[j]) for j in range(chunks)]
    for copy in loads:
        copy.start()
    for load, copy in zip(loads, stores):
        load.wait()
        copy.start()
    for copy in stores:
        copy.wait()


def per_device(
    ncomp,
    nspace,
    spectrum,
    wind_field,
    coupling,
    growth,
    dissipation,
    group_speed,
    refraction,
    depths,
    sea_mask,
    depth_index,
):
    nfreq = growth.shape[0]
    blocks = nfreq // FB
    messages = SUBSTEPS * blocks
    components, points = spectrum.shape
    f32 = jnp.float32
    hbm = pl.BlockSpec(memory_space=pl.ANY)
    dma = pltpu.SemaphoreType.DMA
    moved = pl.pallas_call(
        functools.partial(kernel, nfreq, ncomp, nspace),
        out_shape=jax.ShapeDtypeStruct((components, points), f32),
        in_specs=[hbm] * 10,
        out_specs=hbm,
        scratch_shapes=[
            pltpu.SMEM((4 * ND,), f32),
            pltpu.SMEM(growth.shape, f32),
            pltpu.SMEM(dissipation.shape, f32),
            pltpu.SMEM(depths.shape, f32),
            pltpu.VMEM(wind_field.shape, f32),
            pltpu.VMEM(group_speed.shape, f32),
            pltpu.VMEM(refraction.shape, f32),
            pltpu.VMEM((8, NY), jnp.int32),
            pltpu.VMEM((8, NY), jnp.int32),
            pltpu.VMEM((RB, components, NY), f32),
            pltpu.VMEM((components, components), jnp.bfloat16),
            pltpu.VMEM((components, points), jnp.bfloat16),
            pltpu.VMEM((RB, FB * ND, NY), f32),
            pltpu.VMEM((blocks, ND, RB, FB, NY), f32),
            pltpu.VMEM((ND + 3, RB, FB, NY), f32),
            pltpu.VMEM((RB, components, NY), f32),
            pltpu.VMEM((messages, SLOTS, FB, NY), f32),
            pltpu.VMEM((messages, SLOTS, FB, NY), f32),
            pltpu.VMEM((messages, SLOTS, FB, NY), f32),
            pltpu.VMEM((messages, SLOTS, FB, NY), f32),
            pltpu.VMEM((2, 2, 8, NY), jnp.int32),
            pltpu.VMEM((2, 2, 8, NY), jnp.int32),
            pltpu.VMEM((RB + 1, nfreq, NY), f32),
            pltpu.VMEM((RB, nfreq, NY), f32),
            pltpu.VMEM((RB, nfreq, NY), f32),
            pltpu.VMEM((RB, nfreq, NY), f32),
            pltpu.VMEM((RB, 8, NY), f32),
            pltpu.VMEM((2, 8, points), f32),
            pltpu.VMEM((8, points), f32),
            dma((8,)),
            dma((RB,)),
            dma((blocks,)),
            dma((blocks, RB)),
            dma((messages,)),
            dma((messages,)),
            dma((messages,)),
            dma((messages,)),
            dma((2,)),
            dma((2,)),
        ],
        compiler_params=pltpu.CompilerParams(
            collective_id=0, has_side_effects=True, vmem_limit_bytes=64 * 1024 * 1024 - 4096
        ),
    )(
        spectrum,
        wind_field,
        coupling,
        growth,
        dissipation,
        group_speed,
        refraction,
        depths,
        sea_mask,
        depth_index,
    )
    chunks = 8
    return pl.pallas_call(
        hand_on,
        out_shape=jax.ShapeDtypeStruct((components, points), f32),
        in_specs=[hbm],
        out_specs=hbm,
        scratch_shapes=[dma((chunks,)), dma((chunks,)), pltpu.VMEM((components, points), f32)],
    )(moved)


def solution(mesh):
    in_specs = (
        P(None, ("comp", "space")),
        P(None, ("comp", "space")),
        P(),
        P(),
        P(),
        P(),
        P(),
        P(),
        P("space", None),
        P("space", None),
    )
    out_specs = P(None, ("comp", "space"))
    body = functools.partial(per_device, mesh.shape["comp"], mesh.shape["space"])
    return jax.shard_map(body, mesh=mesh, in_specs=in_specs, out_specs=out_specs, check_vma=False)
```

```python
import functools

import jax
import jax.numpy as jnp
import numpy as np
from jax import lax
from jax.experimental import pallas as pl
from jax.experimental.pallas import tpu as pltpu
from jax.sharding import PartitionSpec as P

ND = 36
NQ = 9
RB = 4
NY = 128
SUBSTEPS = 3
FB = 8
SLOTS = 6 * NQ
LEFT_LAG = 1
PAIRS = ((2, 3), (0, 1))
MESH = pl.DeviceIdType.MESH


def direction_tables():
    angles = np.float32(2.0 * np.pi) * np.arange(ND, dtype=np.float32) / np.float32(ND)
    cosine = np.cos(angles.astype(np.float64)).astype(np.float32)
    sine = np.sin(angles.astype(np.float64)).astype(np.float32)
    half_cos = np.float32(0.5) * (cosine + np.roll(cosine, -1))
    half_sin = np.float32(0.5) * (sine + np.roll(sine, -1))
    return np.concatenate([cosine, sine, half_cos, half_sin])


def face_of(nu, base, diff, second):
    return nu * (base + (1.0 - nu) * (0.5 * diff - (nu * (1.0 / 6.0) + (1.0 / 6.0)) * second))


def kernel(
    nfreq,
    ncomp,
    nspace,
    spectrum,
    wind_hbm,
    coupling,
    growth_hbm,
    dissipation_hbm,
    group_speed_hbm,
    refraction_hbm,
    depths_hbm,
    sea_mask_hbm,
    depth_index_hbm,
    out,
    trig,
    growth,
    dissipation,
    depths,
    wind,
    group_speed,
    refraction,
    sea_mask,
    depth_index,
    spec_v,
    coup_v,
    spec_b,
    nonlin,
    energy,
    work,
    send_l,
    send_r,
    recv_l,
    recv_r,
    coast_out,
    coast_in,
    gx,
    gy,
    rx,
    ry,
    mask_v,
    wind_v,
    ratio_v,
    small_sem,
    load_sem,
    coup_sem,
    send_l_sem,
    send_r_sem,
    recv_l_sem,
    recv_r_sem,
    coast_send_sem,
    coast_recv_sem,
):
    blocks = nfreq // FB
    rows_b = FB * ND
    components = nfreq * ND
    c = lax.axis_index("comp")
    s = lax.axis_index("space")
    total = ncomp * nspace
    n = s * ncomp + c
    before = lax.rem(n + total - 1, total)
    after = lax.rem(n + 1, total)
    left = (lax.rem(before, ncomp), lax.div(before, ncomp))
    right = (lax.rem(after, ncomp), lax.div(after, ncomp))
    edge_l = jnp.where(n > 0, 1.0, 0.0).astype(jnp.float32)
    edge_r = jnp.where(n < total - 1, 1.0, 0.0).astype(jnp.float32)

    barrier = pltpu.get_barrier_semaphore()
    pl.semaphore_signal(barrier, inc=1, device_id=left, device_id_type=MESH)
    pl.semaphore_signal(barrier, inc=1, device_id=right, device_id_type=MESH)

    def lanes(r):
        return slice(r * NY, (r + 1) * NY)

    def spec_load(r):
        return pltpu.make_async_copy(spectrum.at[:, lanes(r)], spec_v.at[r], load_sem.at[r])

    own_tile = pl.ds(pl.multiple_of(lax.div(c * RB, 8) * 8, 8), 8)
    small_loads = [
        pltpu.make_async_copy(src, dst, small_sem.at[j])
        for j, (src, dst) in enumerate(
            (
                (sea_mask_hbm.at[own_tile], sea_mask),
                (depth_index_hbm.at[own_tile], depth_index),
                (wind_hbm, wind),
                (growth_hbm, growth),
                (dissipation_hbm, dissipation),
                (group_speed_hbm, group_speed),
                (refraction_hbm, refraction),
                (depths_hbm, depths),
            )
        )
    ]
    for load in small_loads:
        load.start()

    def coup_load(b):
        rows = pl.ds(pl.multiple_of(b * rows_b, rows_b), rows_b)
        return pltpu.make_async_copy(coupling.at[rows], coup_v.at[rows], coup_sem.at[b])

    coup_load(0).start()
    for r in PAIRS[0]:
        spec_load(r).start()

    for at, value in enumerate(direction_tables()):
        trig[at] = jnp.float32(value)
    for load in small_loads:
        load.wait()

    def to_left(k):
        return pltpu.make_async_remote_copy(
            src_ref=send_l.at[k],
            dst_ref=recv_r.at[k],
            send_sem=send_l_sem.at[k],
            recv_sem=recv_r_sem.at[k],
            device_id=left,
            device_id_type=MESH,
        )

    def to_right(k):
        return pltpu.make_async_remote_copy(
            src_ref=send_r.at[k],
            dst_ref=recv_l.at[k],
            send_sem=send_r_sem.at[k],
            recv_sem=recv_l_sem.at[k],
            device_id=right,
            device_id_type=MESH,
        )

    wind_v[0] = jnp.broadcast_to(wind[0:1, :], (8, RB * NY))
    wind_v[1] = jnp.broadcast_to(wind[1:2, :], (8, RB * NY))

    def pack_right(q, i, k, rows):
        at = i + (0 if q in (0, 1) else NQ)
        if q in (0, 3):
            send_r[k, 2 * at] = rows[RB - 2]
            send_r[k, 2 * at + 1] = rows[RB - 1]
        else:
            send_r[k, 4 * NQ + at] = rows[RB - 1]

    def pack_left(q, i, k, rows):
        at = i + (0 if q in (0, 1) else NQ)
        if q in (0, 3):
            send_l[k, 4 * NQ + at] = rows[0]
        else:
            send_l[k, 2 * at] = rows[0]
            send_l[k, 2 * at + 1] = rows[1]

    sub8 = lax.broadcasted_iota(jnp.int32, (FB, NY), 0)

    def by_freq(table, b):
        values = jnp.zeros((FB, NY), jnp.float32)
        for j in range(FB):
            values = jnp.where(sub8 == j, table[b * FB + j], values)
        return values

    def prepare(r):
        spec_load(r).wait()

        def cast_rows(i, acc):
            rows = pl.ds(pl.multiple_of(i * 64, 64), 64)
            block = spec_v[r, rows, :]
            spec_b[rows, lanes(r)] = block.astype(jnp.bfloat16)
            return acc + jnp.sum(block.reshape(8, 8, NY), axis=0)

        acc = lax.fori_loop(0, components // 64, cast_rows, jnp.zeros((8, NY), jnp.float32))
        average = jnp.sum(acc, axis=0, keepdims=True) * (1.0 / components)
        ratio_v[:, lanes(r)] = jnp.broadcast_to(average / (average + 1.0), (8, NY))

    def source(b, pair):
        rows = pl.ds(pl.multiple_of(b * rows_b, rows_b), rows_b)
        columns = slice(pair[0] * NY, (pair[-1] + 1) * NY)
        product = jnp.dot(coup_v[rows, :], spec_b[:, columns], preferred_element_type=jnp.float32)
        for at, r in enumerate(pair):
            nonlin[r] = product[:, lanes(at)]
        grow = by_freq(growth, b)
        damp = by_freq(dissipation, b)
        damps = {r: damp * ratio_v[:, lanes(r)] for r in pair}

        def directions(i, inner):
            for q in range(4):
                d = q * NQ + i
                cosine = trig[d]
                sine = trig[ND + d]
                made = {}
                for r in pair:
                    forcing = jnp.maximum(cosine * wind_v[0, :, lanes(r)] + sine * wind_v[1, :, lanes(r)], 0.0)
                    value = spec_v[r, pl.ds(b * rows_b + d, FB, stride=ND), :]
                    extra = nonlin[r, pl.ds(d, FB, stride=ND), :]
                    value = value + (grow * (forcing * forcing) - damps[r]) * value + 0.25 * extra
                    energy[b, d, r] = value
                    made[r] = value
                if pair == PAIRS[0]:
                    pack_right(q, i, b, made)
                else:
                    pack_left(q, i, b, made)
            return inner

        lax.fori_loop(0, NQ, directions, 0, unroll=3)

    def source_right(b, carry):
        coup_load(b).wait()
        source(b, PAIRS[0])
        to_right(b).start()
        return carry

    def source_left(b, carry):
        source(b, PAIRS[1])
        to_left(b).start()
        return carry

    def source_both(b, carry):
        return source_left(b - LEFT_LAG, source_right(b, carry))

    prepare(PAIRS[0][0])
    for r in PAIRS[1]:
        spec_load(r).start()
    prepare(PAIRS[0][1])
    coup_load(0).wait()
    source(0, PAIRS[0])

    row0 = lax.rem(c * RB, 8)
    own_mask = [sea_mask[pl.ds(row0 + r, 1), :] for r in range(RB)]
    own_index = [depth_index[pl.ds(row0 + r, 1), :] for r in range(RB)]
    for side, r in ((0, 0), (1, RB - 1)):
        coast_out[side, 0] = jnp.broadcast_to(own_mask[r], (8, NY))
        coast_out[side, 1] = jnp.broadcast_to(own_index[r], (8, NY))

    pl.semaphore_wait(barrier, 2)

    def coast_copy(side):
        return pltpu.make_async_remote_copy(
            src_ref=coast_out.at[side],
            dst_ref=coast_in.at[1 - side],
            send_sem=coast_send_sem.at[side],
            recv_sem=coast_recv_sem.at[1 - side],
            device_id=left if side == 0 else right,
            device_id_type=MESH,
        )

    for side in range(2):
        coast_copy(side).start()

    to_right(0).start()
    for b in range(1, blocks):
        coup_load(b).start()
    lax.fori_loop(1, LEFT_LAG, source_right, 0)
    for r in PAIRS[1]:
        prepare(r)
    lax.fori_loop(LEFT_LAG, blocks, source_both, 0)
    lax.fori_loop(blocks - LEFT_LAG, blocks, source_left, 0)

    for side in range(2):
        coast_copy(side).wait()
    mask_rows = (
        [coast_in[0, 0, 0:1, :].astype(jnp.float32) * edge_l]
        + [m.astype(jnp.float32) for m in own_mask]
        + [coast_in[1, 0, 0:1, :].astype(jnp.float32) * edge_r]
    )
    index_rows = [coast_in[0, 1, 0:1, :]] + own_index + [coast_in[1, 1, 0:1, :]]
    levels = depths.shape[0]
    level = lax.broadcasted_iota(jnp.int32, (levels, NY), 0)
    onehot = jnp.concatenate(
        [(jnp.broadcast_to(row, (levels, NY)) == level).astype(jnp.float32) for row in index_rows], axis=1
    )
    speeds = jnp.dot(
        group_speed[...], onehot, precision=lax.Precision.HIGHEST, preferred_element_type=jnp.float32
    )
    turning = jnp.dot(
        refraction[...],
        onehot[:, NY : (RB + 1) * NY],
        precision=lax.Precision.HIGHEST,
        preferred_element_type=jnp.float32,
    )
    lane_row = lax.broadcasted_iota(jnp.int32, (1, NY), 1)
    heights = []
    for row, mask in zip(index_rows, mask_rows):
        height = jnp.zeros((1, NY), jnp.float32)
        for entry in range(levels):
            height = jnp.where(row == entry, depths[entry], height)
        heights.append(height * mask)
    for j in range(RB + 1):
        pair = 0.5 * (speeds[:, lanes(j)] + speeds[:, lanes(j + 1)])
        gx[j] = pair * (mask_rows[j] * mask_rows[j + 1])
    for r in range(RB):
        mask = mask_rows[r + 1]
        own = speeds[:, lanes(r + 1)]
        beyond = jnp.where(lane_row == NY - 1, 0.0, pltpu.roll(jnp.broadcast_to(mask, (8, NY)), NY - 1, 1)[:1])
        gy[r] = 0.5 * (own + pltpu.roll(own, NY - 1, 1)) * (mask * beyond)
        wide = jnp.broadcast_to(heights[r + 1], (8, NY))
        up = jnp.where(lane_row == NY - 1, 0.0, pltpu.roll(wide, NY - 1, 1)[:1])
        down = jnp.where(lane_row == 0, 0.0, pltpu.roll(wide, 1, 1)[:1])
        rx[r] = turning[:, lanes(r)] * (0.5 * (heights[r + 2] - heights[r]))
        ry[r] = turning[:, lanes(r)] * (0.5 * (up - down))
        mask_v[r] = jnp.broadcast_to(mask, (8, NY))


    lane8 = lax.broadcasted_iota(jnp.int32, (FB, NY), 1)
    first_lane = lane8 == 0
    last_lanes = lane8 >= NY - 2

    def passes(k, b, emit):
        to_left(k).wait_recv()
        to_right(k).wait_recv()
        freqs = pl.ds(pl.multiple_of(b * FB, FB), FB)

        def along_x_and_y(i, carry):
            for q in range(4):
                d = q * NQ + i
                cosine = trig[d]
                sine = trig[ND + d]
                own = [energy[b, d, r] for r in range(RB)]
                at = i + (0 if q in (0, 1) else NQ)
                if q in (0, 3):
                    ext = [recv_l[k, 2 * at] * edge_l, recv_l[k, 2 * at + 1] * edge_l]
                    ext = ext + own + [recv_r[k, 4 * NQ + at] * edge_r]
                    shift = 1
                else:
                    ext = [recv_l[k, 4 * NQ + at] * edge_l] + own
                    ext = ext + [recv_r[k, 2 * at] * edge_r, recv_r[k, 2 * at + 1] * edge_r]
                    shift = 0
                diff = [ext[j + 1] - ext[j] for j in range(RB + 2)]
                second = [diff[j + 1] - diff[j] for j in range(RB + 1)]
                faces = []
                for j in range(RB + 1):
                    nu = cosine * gx[j, freqs, :]
                    faces.append(face_of(nu, ext[j + shift], diff[j + shift], second[j]))
                for r in range(RB):
                    value = own[r] - (faces[r + 1] - faces[r])
                    nu = sine * gy[r, freqs, :]
                    if q in (0, 1):
                        behind = value - jnp.where(first_lane, 0.0, pltpu.roll(value, 1, 1))
                        ahead = pltpu.roll(value, NY - 1, 1) - value
                        face = face_of(nu, value, ahead, ahead - behind)
                    else:
                        next1 = pltpu.roll(value, NY - 1, 1)
                        next2 = jnp.where(last_lanes, 0.0, pltpu.roll(value, NY - 2, 1))
                        ahead = next1 - value
                        face = face_of(nu, value, ahead, next2 - next1 - ahead)
                    work[d + 1, r] = value - (face - pltpu.roll(face, 1, 1))
            return carry

        lax.fori_loop(0, NQ, along_x_and_y, 0, unroll=3)
        for r in range(RB):
            work[0, r] = work[ND, r]
            work[ND + 1, r] = work[1, r]
            work[ND + 2, r] = work[2, r]

        def turn_face(d, r, base, diff, second, second_next):
            nu = trig[3 * ND + d] * rx[r, freqs, :] - trig[2 * ND + d] * ry[r, freqs, :]
            return face_of(nu, base, diff, jnp.where(nu >= 0.0, second, second_next))

        carry = []
        for r in range(RB):
            e34, e35, e0, e1 = work[ND - 1, r], work[ND, r], work[1, r], work[2, r]
            d34, d35, d0 = e35 - e34, e0 - e35, e1 - e0
            face = turn_face(ND - 1, r, e35, d35, d35 - d34, d0 - d35)
            carry.append((e0, e1, d0, d0 - d35, face))
        carry = tuple(carry)
        for q in range(4):

            def along_directions(i, state, q=q):
                d = q * NQ + i
                made = []
                later = []
                for r in range(RB):
                    e0, e1, diff, second, face_before = state[r]
                    e2 = work[d + 3, r]
                    diff_next = e2 - e1
                    second_next = diff_next - diff
                    face = turn_face(d, r, e0, diff, second, second_next)
                    made.append((e0 - (face - face_before)) * mask_v[r])
                    later.append((e1, e2, diff_next, second_next, face))
                emit(q, i, d, made)
                return tuple(later)

            carry = lax.fori_loop(0, NQ, along_directions, carry, unroll=3)

    def middle(k, carry):
        b = lax.rem(k, blocks)

        def emit(q, i, d, rows):
            for r in range(RB):
                energy[b, d, r] = rows[r]
            pack_right(q, i, k + blocks, rows)
            pack_left(q, i, k + blocks, rows)

        passes(k, b, emit)
        to_right(k + blocks).start()
        to_left(k + blocks).start()
        return carry

    lax.fori_loop(0, (SUBSTEPS - 1) * blocks, middle, 0)

    def final(b, carry):
        def emit(q, i, d, rows):
            for r in range(RB):
                out[r, pl.ds(b * rows_b + d, FB, stride=ND), :] = rows[r]

        passes(b + (SUBSTEPS - 1) * blocks, b, emit)
        return carry

    lax.fori_loop(0, blocks, final, 0)

    def drain(k, carry):
        to_left(k).wait_send()
        to_right(k).wait_send()
        return carry

    lax.fori_loop(0, SUBSTEPS * blocks, drain, 0)


def hand_on(moved, out, sems):
    chunks = sems.shape[1]
    rows = moved.shape[1] // chunks
    copies = [
        pltpu.make_async_copy(
            moved.at[r, pl.ds(j * rows, rows)],
            out.at[pl.ds(j * rows, rows), r * NY : (r + 1) * NY],
            sems.at[r, j],
        )
        for r in range(RB)
        for j in range(chunks)
    ]
    for copy in copies:
        copy.start()
    for copy in copies:
        copy.wait()


def per_device(
    ncomp,
    nspace,
    spectrum,
    wind_field,
    coupling,
    growth,
    dissipation,
    group_speed,
    refraction,
    depths,
    sea_mask,
    depth_index,
):
    nfreq = growth.shape[0]
    blocks = nfreq // FB
    messages = SUBSTEPS * blocks
    components, points = spectrum.shape
    f32 = jnp.float32
    hbm = pl.BlockSpec(memory_space=pl.ANY)
    dma = pltpu.SemaphoreType.DMA
    moved = pl.pallas_call(
        functools.partial(kernel, nfreq, ncomp, nspace),
        out_shape=pltpu.VMEM((RB, components, NY), f32),
        in_specs=[hbm] * 10,
        out_specs=pl.BlockSpec(memory_space=pltpu.VMEM),
        scratch_shapes=[
            pltpu.SMEM((4 * ND,), f32),
            pltpu.SMEM(growth.shape, f32),
            pltpu.SMEM(dissipation.shape, f32),
            pltpu.SMEM(depths.shape, f32),
            pltpu.VMEM(wind_field.shape, f32),
            pltpu.VMEM(group_speed.shape, f32),
            pltpu.VMEM(refraction.shape, f32),
            pltpu.VMEM((8, NY), jnp.int32),
            pltpu.VMEM((8, NY), jnp.int32),
            pltpu.VMEM((RB, components, NY), f32),
            pltpu.VMEM((components, components), jnp.bfloat16),
            pltpu.VMEM((components, points), jnp.bfloat16),
            pltpu.VMEM((RB, FB * ND, NY), f32),
            pltpu.VMEM((blocks, ND, RB, FB, NY), f32),
            pltpu.VMEM((ND + 3, RB, FB, NY), f32),
            pltpu.VMEM((messages, SLOTS, FB, NY), f32),
            pltpu.VMEM((messages, SLOTS, FB, NY), f32),
            pltpu.VMEM((messages, SLOTS, FB, NY), f32),
            pltpu.VMEM((messages, SLOTS, FB, NY), f32),
            pltpu.VMEM((2, 2, 8, NY), jnp.int32),
            pltpu.VMEM((2, 2, 8, NY), jnp.int32),
            pltpu.VMEM((RB + 1, nfreq, NY), f32),
            pltpu.VMEM((RB, nfreq, NY), f32),
            pltpu.VMEM((RB, nfreq, NY), f32),
            pltpu.VMEM((RB, nfreq, NY), f32),
            pltpu.VMEM((RB, 8, NY), f32),
            pltpu.VMEM((2, 8, points), f32),
            pltpu.VMEM((8, points), f32),
            dma((8,)),
            dma((RB,)),
            dma((blocks,)),
            dma((messages,)),
            dma((messages,)),
            dma((messages,)),
            dma((messages,)),
            dma((2,)),
            dma((2,)),
        ],
        compiler_params=pltpu.CompilerParams(
            collective_id=0, has_side_effects=True, vmem_limit_bytes=48 * 1024 * 1024
        ),
    )(
        *[
            pltpu.with_memory_space_constraint(operand, pltpu.HBM)
            for operand in (
                spectrum,
                wind_field,
                coupling,
                growth,
                dissipation,
                group_speed,
                refraction,
                depths,
                sea_mask,
                depth_index,
            )
        ]
    )
    return pl.pallas_call(
        hand_on,
        out_shape=jax.ShapeDtypeStruct((components, points), f32),
        in_specs=[pl.BlockSpec(memory_space=pltpu.VMEM)],
        out_specs=hbm,
        scratch_shapes=[dma((RB, 1))],
    )(pltpu.with_memory_space_constraint(moved, pltpu.VMEM))


def solution(mesh):
    in_specs = (
        P(None, ("comp", "space")),
        P(None, ("comp", "space")),
        P(),
        P(),
        P(),
        P(),
        P(),
        P(),
        P("space", None),
        P("space", None),
    )
    out_specs = P(None, ("comp", "space"))
    body = functools.partial(per_device, mesh.shape["comp"], mesh.shape["space"])
    return jax.shard_map(body, mesh=mesh, in_specs=in_specs, out_specs=out_specs, check_vma=False)
```

```python
import functools

import jax
import jax.numpy as jnp
import numpy as np
from jax import lax
from jax.experimental import pallas as pl
from jax.experimental.pallas import tpu as pltpu
from jax.sharding import PartitionSpec as P

ND = 36
NQ = 9
RB = 4
NY = 128
SUBSTEPS = 3
FB = 8
SLOTS = 6 * NQ
LOW, HIGH = (0, 1), (2, 3)
LINE = 8
RIGHT_AT = (0, 2 * NQ, 3 * NQ, 4 * NQ, 6 * NQ)
LEFT_AT = (0, NQ, 3 * NQ, 5 * NQ, 6 * NQ)
MESH = pl.DeviceIdType.MESH


def direction_tables():
    angles = np.float32(2.0 * np.pi) * np.arange(ND, dtype=np.float32) / np.float32(ND)
    cosine = np.cos(angles.astype(np.float64)).astype(np.float32)
    sine = np.sin(angles.astype(np.float64)).astype(np.float32)
    half_cos = np.float32(0.5) * (cosine + np.roll(cosine, -1))
    half_sin = np.float32(0.5) * (sine + np.roll(sine, -1))
    return np.concatenate([cosine, sine, half_cos, half_sin])


def face_of(nu, base, diff, second):
    return nu * (base + (1.0 - nu) * (0.5 * diff - (nu * (1.0 / 6.0) + (1.0 / 6.0)) * second))


def kernel(
    nfreq,
    ncomp,
    nspace,
    spectrum,
    wind_hbm,
    coupling,
    growth_hbm,
    dissipation_hbm,
    group_speed_hbm,
    refraction_hbm,
    depths_hbm,
    sea_mask_hbm,
    depth_index_hbm,
    out,
    trig,
    growth,
    dissipation,
    depths,
    wind,
    group_speed,
    refraction,
    sea_mask,
    depth_index,
    spec_v,
    coup_v,
    spec_b,
    nonlin,
    energy,
    work,
    send_l,
    send_r,
    recv_l,
    recv_r,
    coast_out,
    coast_in,
    gx,
    gy,
    rx,
    ry,
    mask_v,
    wind_v,
    ratio_v,
    small_sem,
    load_sem,
    coup_sem,
    send_l_sem,
    send_r_sem,
    recv_l_sem,
    recv_r_sem,
    part_send_l_sem,
    part_send_r_sem,
    part_recv_l_sem,
    part_recv_r_sem,
    coast_send_sem,
    coast_recv_sem,
):
    blocks = nfreq // FB
    rows_b = FB * ND
    components = nfreq * ND
    c = lax.axis_index("comp")
    s = lax.axis_index("space")
    total = ncomp * nspace
    n = s * ncomp + c
    before = lax.rem(n + total - 1, total)
    after = lax.rem(n + 1, total)
    left = (lax.rem(before, ncomp), lax.div(before, ncomp))
    right = (lax.rem(after, ncomp), lax.div(after, ncomp))
    edge_l = jnp.where(n > 0, 1.0, 0.0).astype(jnp.float32)
    edge_r = jnp.where(n < total - 1, 1.0, 0.0).astype(jnp.float32)

    barrier = pltpu.get_barrier_semaphore()
    pl.semaphore_signal(barrier, inc=1, device_id=left, device_id_type=MESH)
    pl.semaphore_signal(barrier, inc=1, device_id=right, device_id_type=MESH)

    def lanes(r):
        return slice(r * NY, (r + 1) * NY)

    def spec_load(r):
        return pltpu.make_async_copy(spectrum.at[:, lanes(r)], spec_v.at[r], load_sem.at[r])

    own_tile = pl.ds(pl.multiple_of(lax.div(c * RB, 8) * 8, 8), 8)
    small_loads = [
        pltpu.make_async_copy(src, dst, small_sem.at[j])
        for j, (src, dst) in enumerate(
            (
                (sea_mask_hbm.at[own_tile], sea_mask),
                (depth_index_hbm.at[own_tile], depth_index),
                (wind_hbm, wind),
                (growth_hbm, growth),
                (dissipation_hbm, dissipation),
                (group_speed_hbm, group_speed),
                (refraction_hbm, refraction),
                (depths_hbm, depths),
            )
        )
    ]
    for load in small_loads:
        load.start()

    def coup_load(b):
        rows = pl.ds(pl.multiple_of(b * rows_b, rows_b), rows_b)
        return pltpu.make_async_copy(coupling.at[rows], coup_v.at[rows], coup_sem.at[b])

    coup_load(0).start()

    for at, value in enumerate(direction_tables()):
        trig[at] = jnp.float32(value)
    for load in small_loads:
        load.wait()

    def to_left(k):
        return pltpu.make_async_remote_copy(
            src_ref=send_l.at[k],
            dst_ref=recv_r.at[k],
            send_sem=send_l_sem.at[k],
            recv_sem=recv_r_sem.at[k],
            device_id=left,
            device_id_type=MESH,
        )

    def to_right(k):
        return pltpu.make_async_remote_copy(
            src_ref=send_r.at[k],
            dst_ref=recv_l.at[k],
            send_sem=send_r_sem.at[k],
            recv_sem=recv_l_sem.at[k],
            device_id=right,
            device_id_type=MESH,
        )

    wind_v[0] = jnp.broadcast_to(wind[0:1, :], (8, RB * NY))
    wind_v[1] = jnp.broadcast_to(wind[1:2, :], (8, RB * NY))

    def pack_right(q, i, k, rows):
        at = RIGHT_AT[q]
        if q in (0, 3):
            send_r[k, at + 2 * i] = rows[RB - 2]
            send_r[k, at + 2 * i + 1] = rows[RB - 1]
        else:
            send_r[k, at + i] = rows[RB - 1]

    def pack_left(q, i, k, rows):
        at = LEFT_AT[q]
        if q in (0, 3):
            send_l[k, at + i] = rows[0]
        else:
            send_l[k, at + 2 * i] = rows[0]
            send_l[k, at + 2 * i + 1] = rows[1]

    sub8 = lax.broadcasted_iota(jnp.int32, (FB, NY), 0)

    def by_freq(table, b):
        values = jnp.zeros((FB, NY), jnp.float32)
        for j in range(FB):
            values = jnp.where(sub8 == j, table[b * FB + j], values)
        return values

    last = SUBSTEPS * blocks - 1

    def left_part(q):
        tiles = pl.ds(LEFT_AT[q], LEFT_AT[q + 1] - LEFT_AT[q])
        return pltpu.make_async_remote_copy(
            src_ref=send_l.at[last, tiles],
            dst_ref=recv_r.at[last, tiles],
            send_sem=part_send_l_sem.at[q],
            recv_sem=part_recv_r_sem.at[q],
            device_id=left,
            device_id_type=MESH,
        )

    def right_part(q):
        tiles = pl.ds(RIGHT_AT[q], RIGHT_AT[q + 1] - RIGHT_AT[q])
        return pltpu.make_async_remote_copy(
            src_ref=send_r.at[last, tiles],
            dst_ref=recv_l.at[last, tiles],
            send_sem=part_send_r_sem.at[q],
            recv_sem=part_recv_l_sem.at[q],
            device_id=right,
            device_id_type=MESH,
        )

    def prepare(r):
        spec_load(r).wait()

        def cast_rows(i, acc):
            rows = pl.ds(pl.multiple_of(i * 64, 64), 64)
            block = spec_v[r, rows, :]
            spec_b[rows, lanes(r)] = block.astype(jnp.bfloat16)
            return acc + jnp.sum(block.reshape(8, 8, NY), axis=0)

        acc = lax.fori_loop(0, components // 64, cast_rows, jnp.zeros((8, NY), jnp.float32))
        average = jnp.sum(acc, axis=0, keepdims=True) * (1.0 / components)
        ratio_v[:, lanes(r)] = jnp.broadcast_to(average / (average + 1.0), (8, NY))

    def source(b, pair):
        rows = pl.ds(pl.multiple_of(b * rows_b, rows_b), rows_b)
        columns = slice(pair[0] * NY, (pair[-1] + 1) * NY)
        product = jnp.dot(coup_v[rows, :], spec_b[:, columns], preferred_element_type=jnp.float32)
        for at, r in enumerate(pair):
            nonlin[r] = product[:, lanes(at)]
        grow = by_freq(growth, b)
        damp = by_freq(dissipation, b)
        damps = {r: damp * ratio_v[:, lanes(r)] for r in pair}

        def directions(i, inner):
            for q in range(4):
                d = q * NQ + i
                cosine = trig[d]
                sine = trig[ND + d]
                made = {}
                for r in pair:
                    forcing = jnp.maximum(cosine * wind_v[0, :, lanes(r)] + sine * wind_v[1, :, lanes(r)], 0.0)
                    value = spec_v[r, pl.ds(b * rows_b + d, FB, stride=ND), :]
                    extra = nonlin[r, pl.ds(d, FB, stride=ND), :]
                    value = value + (grow * (forcing * forcing) - damps[r]) * value + 0.25 * extra
                    energy[b, d, r] = value
                    made[r] = value
                if pair == HIGH:
                    pack_right(q, i, b, made)
                else:
                    pack_left(q, i, b, made)
            return inner

        lax.fori_loop(0, NQ, directions, 0, unroll=3)

    def open_with(first, second):
        for r in first:
            spec_load(r).start()
        prepare(first[0])
        for r in second:
            spec_load(r).start()
        prepare(first[1])
        coup_load(0).wait()
        source(0, first)

    def go_on_with(first, second):
        send_of(first, 0).start()
        for r in second:
            prepare(r)
        for b in range(1, blocks):
            coup_load(b).start()
        source(0, second)
        send_of(second, 0).start()

        def others(b, carry):
            coup_load(b).wait()
            source(b, first)
            send_of(first, b).start()
            source(b, second)
            send_of(second, b).start()
            return carry

        lax.fori_loop(1, blocks, others, 0)

    def send_of(pair, k):
        return to_left(k) if pair == LOW else to_right(k)

    low_first = jnp.logical_and(lax.rem(c, 2) == 0, c < ncomp - LINE)
    pl.when(low_first)(lambda: open_with(LOW, HIGH))
    pl.when(jnp.logical_not(low_first))(lambda: open_with(HIGH, LOW))

    row0 = lax.rem(c * RB, 8)
    own_mask = [sea_mask[pl.ds(row0 + r, 1), :] for r in range(RB)]
    own_index = [depth_index[pl.ds(row0 + r, 1), :] for r in range(RB)]
    for side, r in ((0, 0), (1, RB - 1)):
        coast_out[side, 0] = jnp.broadcast_to(own_mask[r], (8, NY))
        coast_out[side, 1] = jnp.broadcast_to(own_index[r], (8, NY))

    pl.semaphore_wait(barrier, 2)

    def coast_copy(side):
        return pltpu.make_async_remote_copy(
            src_ref=coast_out.at[side],
            dst_ref=coast_in.at[1 - side],
            send_sem=coast_send_sem.at[side],
            recv_sem=coast_recv_sem.at[1 - side],
            device_id=left if side == 0 else right,
            device_id_type=MESH,
        )

    for side in range(2):
        coast_copy(side).start()

    pl.when(low_first)(lambda: go_on_with(LOW, HIGH))
    pl.when(jnp.logical_not(low_first))(lambda: go_on_with(HIGH, LOW))

    for side in range(2):
        coast_copy(side).wait()
    mask_rows = (
        [coast_in[0, 0, 0:1, :].astype(jnp.float32) * edge_l]
        + [m.astype(jnp.float32) for m in own_mask]
        + [coast_in[1, 0, 0:1, :].astype(jnp.float32) * edge_r]
    )
    index_rows = [coast_in[0, 1, 0:1, :]] + own_index + [coast_in[1, 1, 0:1, :]]
    levels = depths.shape[0]
    level = lax.broadcasted_iota(jnp.int32, (levels, NY), 0)
    onehot = jnp.concatenate(
        [(jnp.broadcast_to(row, (levels, NY)) == level).astype(jnp.float32) for row in index_rows], axis=1
    )
    speeds = jnp.dot(
        group_speed[...], onehot, precision=lax.Precision.HIGHEST, preferred_element_type=jnp.float32
    )
    turning = jnp.dot(
        refraction[...],
        onehot[:, NY : (RB + 1) * NY],
        precision=lax.Precision.HIGHEST,
        preferred_element_type=jnp.float32,
    )
    lane_row = lax.broadcasted_iota(jnp.int32, (1, NY), 1)
    heights = []
    for row, mask in zip(index_rows, mask_rows):
        height = jnp.zeros((1, NY), jnp.float32)
        for entry in range(levels):
            height = jnp.where(row == entry, depths[entry], height)
        heights.append(height * mask)
    for j in range(RB + 1):
        pair = 0.5 * (speeds[:, lanes(j)] + speeds[:, lanes(j + 1)])
        gx[j] = pair * (mask_rows[j] * mask_rows[j + 1])
    for r in range(RB):
        mask = mask_rows[r + 1]
        own = speeds[:, lanes(r + 1)]
        beyond = jnp.where(lane_row == NY - 1, 0.0, pltpu.roll(jnp.broadcast_to(mask, (8, NY)), NY - 1, 1)[:1])
        gy[r] = 0.5 * (own + pltpu.roll(own, NY - 1, 1)) * (mask * beyond)
        wide = jnp.broadcast_to(heights[r + 1], (8, NY))
        up = jnp.where(lane_row == NY - 1, 0.0, pltpu.roll(wide, NY - 1, 1)[:1])
        down = jnp.where(lane_row == 0, 0.0, pltpu.roll(wide, 1, 1)[:1])
        rx[r] = turning[:, lanes(r)] * (0.5 * (heights[r + 2] - heights[r]))
        ry[r] = turning[:, lanes(r)] * (0.5 * (up - down))
        mask_v[r] = jnp.broadcast_to(mask, (8, NY))


    lane8 = lax.broadcasted_iota(jnp.int32, (FB, NY), 1)
    first_lane = lane8 == 0
    last_lanes = lane8 >= NY - 2

    def turn_face(freqs, d, r, base, diff, second, second_next):
        nu = trig[3 * ND + d] * rx[r, freqs, :] - trig[2 * ND + d] * ry[r, freqs, :]
        return face_of(nu, base, diff, jnp.where(nu >= 0.0, second, second_next))

    def last_passes(freqs, arrive, one_quadrant, emit):
        state = None
        cell = 2
        for q in range(4):
            arrive(q)
            one_quadrant(q)
            if q == 3:
                for d in range(4):
                    for r in range(RB):
                        work[ND + 1 + d, r] = work[1 + d, r]
            if q == 0:
                state = []
                for r in range(RB):
                    e0, e1, e2, e3 = (work[1 + d, r] for d in range(4))
                    d0, d1, d2 = e1 - e0, e2 - e1, e3 - e2
                    face = turn_face(freqs, 1, r, e1, d1, d1 - d0, d2 - d1)
                    state.append((e2, e3, d2, d2 - d1, face))
            until = (q + 1) * NQ - 2 if q < 3 else ND + 2
            while cell < until:
                made = []
                for r in range(RB):
                    e0, e1, diff, second, face_before = state[r]
                    e2 = work[cell + 3, r]
                    diff_next = e2 - e1
                    second_next = diff_next - diff
                    face = turn_face(freqs, cell % ND, r, e0, diff, second, second_next)
                    made.append((e0 - (face - face_before)) * mask_v[r])
                    state[r] = (e1, e2, diff_next, second_next, face)
                emit(None, None, cell % ND, made)
                cell += 1

    def passes(k, b, emit, arrive=None):
        if arrive is None:
            to_left(k).wait_recv()
            to_right(k).wait_recv()
        freqs = pl.ds(pl.multiple_of(b * FB, FB), FB)

        def x_and_y(q, i):
            d = q * NQ + i
            cosine = trig[d]
            sine = trig[ND + d]
            own = [energy[b, d, r] for r in range(RB)]
            low, high = RIGHT_AT[q], LEFT_AT[q]
            if q in (0, 3):
                ext = [recv_l[k, low + 2 * i] * edge_l, recv_l[k, low + 2 * i + 1] * edge_l]
                ext = ext + own + [recv_r[k, high + i] * edge_r]
                shift = 1
            else:
                ext = [recv_l[k, low + i] * edge_l] + own
                ext = ext + [recv_r[k, high + 2 * i] * edge_r, recv_r[k, high + 2 * i + 1] * edge_r]
                shift = 0
            diff = [ext[j + 1] - ext[j] for j in range(RB + 2)]
            second = [diff[j + 1] - diff[j] for j in range(RB + 1)]
            faces = []
            for j in range(RB + 1):
                nu = cosine * gx[j, freqs, :]
                faces.append(face_of(nu, ext[j + shift], diff[j + shift], second[j]))
            for r in range(RB):
                value = own[r] - (faces[r + 1] - faces[r])
                nu = sine * gy[r, freqs, :]
                if q in (0, 1):
                    behind = value - jnp.where(first_lane, 0.0, pltpu.roll(value, 1, 1))
                    ahead = pltpu.roll(value, NY - 1, 1) - value
                    face = face_of(nu, value, ahead, ahead - behind)
                else:
                    next1 = pltpu.roll(value, NY - 1, 1)
                    next2 = jnp.where(last_lanes, 0.0, pltpu.roll(value, NY - 2, 1))
                    ahead = next1 - value
                    face = face_of(nu, value, ahead, next2 - next1 - ahead)
                work[d + 1, r] = value - (face - pltpu.roll(face, 1, 1))

        def along_x_and_y(i, carry):
            for q in range(4):
                x_and_y(q, i)
            return carry

        def one_quadrant(q):
            def run(i, carry):
                x_and_y(q, i)
                return carry

            lax.fori_loop(0, NQ, run, 0, unroll=NQ)

        if arrive is not None:
            last_passes(freqs, arrive, one_quadrant, emit)
            return
        lax.fori_loop(0, NQ, along_x_and_y, 0, unroll=3)
        for r in range(RB):
            work[0, r] = work[ND, r]
            work[ND + 1, r] = work[1, r]
            work[ND + 2, r] = work[2, r]

        carry = []
        for r in range(RB):
            e34, e35, e0, e1 = work[ND - 1, r], work[ND, r], work[1, r], work[2, r]
            d34, d35, d0 = e35 - e34, e0 - e35, e1 - e0
            face = turn_face(freqs, ND - 1, r, e35, d35, d35 - d34, d0 - d35)
            carry.append((e0, e1, d0, d0 - d35, face))
        carry = tuple(carry)
        for q in range(4):

            def along_directions(i, state, q=q):
                d = q * NQ + i
                made = []
                later = []
                for r in range(RB):
                    e0, e1, diff, second, face_before = state[r]
                    e2 = work[d + 3, r]
                    diff_next = e2 - e1
                    second_next = diff_next - diff
                    face = turn_face(freqs, d, r, e0, diff, second, second_next)
                    made.append((e0 - (face - face_before)) * mask_v[r])
                    later.append((e1, e2, diff_next, second_next, face))
                emit(q, i, d, made)
                return tuple(later)

            carry = lax.fori_loop(0, NQ, along_directions, carry, unroll=3)

    def middle(k, carry):
        b = lax.rem(k, blocks)

        def emit(q, i, d, rows):
            for r in range(RB):
                energy[b, d, r] = rows[r]
            pack_right(q, i, k + blocks, rows)
            pack_left(q, i, k + blocks, rows)

        passes(k, b, emit)

        @pl.when(k + blocks < last)
        def _():
            to_right(k + blocks).start()
            to_left(k + blocks).start()

        @pl.when(k + blocks == last)
        def _():
            for q in range(4):
                right_part(q).start()
                left_part(q).start()

        return carry

    lax.fori_loop(0, (SUBSTEPS - 1) * blocks, middle, 0)

    def emit_out(b):
        def emit(q, i, d, rows):
            for r in range(RB):
                out[r, pl.ds(b * rows_b + d, FB, stride=ND), :] = rows[r]

        return emit

    def final(b, carry):
        passes(b + (SUBSTEPS - 1) * blocks, b, emit_out(b))
        return carry

    def arrive(q):
        left_part(q).wait_recv()
        right_part(q).wait_recv()

    lax.fori_loop(0, blocks - 1, final, 0)
    passes(last, blocks - 1, emit_out(blocks - 1), arrive)

    def drain(k, carry):
        to_left(k).wait_send()
        to_right(k).wait_send()
        return carry

    lax.fori_loop(0, last, drain, 0)
    for q in range(4):
        left_part(q).wait_send()
        right_part(q).wait_send()


def hand_on(moved, out, sems):
    chunks = sems.shape[1]
    rows = moved.shape[1] // chunks
    copies = [
        pltpu.make_async_copy(
            moved.at[r, pl.ds(j * rows, rows)],
            out.at[pl.ds(j * rows, rows), r * NY : (r + 1) * NY],
            sems.at[r, j],
        )
        for r in range(RB)
        for j in range(chunks)
    ]
    for copy in copies:
        copy.start()
    for copy in copies:
        copy.wait()


def per_device(
    ncomp,
    nspace,
    spectrum,
    wind_field,
    coupling,
    growth,
    dissipation,
    group_speed,
    refraction,
    depths,
    sea_mask,
    depth_index,
):
    nfreq = growth.shape[0]
    blocks = nfreq // FB
    messages = SUBSTEPS * blocks
    components, points = spectrum.shape
    f32 = jnp.float32
    hbm = pl.BlockSpec(memory_space=pl.ANY)
    dma = pltpu.SemaphoreType.DMA
    moved = pl.pallas_call(
        functools.partial(kernel, nfreq, ncomp, nspace),
        out_shape=pltpu.VMEM((RB, components, NY), f32),
        in_specs=[hbm] * 10,
        out_specs=pl.BlockSpec(memory_space=pltpu.VMEM),
        scratch_shapes=[
            pltpu.SMEM((4 * ND,), f32),
            pltpu.SMEM(growth.shape, f32),
            pltpu.SMEM(dissipation.shape, f32),
            pltpu.SMEM(depths.shape, f32),
            pltpu.VMEM(wind_field.shape, f32),
            pltpu.VMEM(group_speed.shape, f32),
            pltpu.VMEM(refraction.shape, f32),
            pltpu.VMEM((8, NY), jnp.int32),
            pltpu.VMEM((8, NY), jnp.int32),
            pltpu.VMEM((RB, components, NY), f32),
            pltpu.VMEM((components, components), jnp.bfloat16),
            pltpu.VMEM((components, points), jnp.bfloat16),
            pltpu.VMEM((RB, FB * ND, NY), f32),
            pltpu.VMEM((blocks, ND, RB, FB, NY), f32),
            pltpu.VMEM((ND + 5, RB, FB, NY), f32),
            pltpu.VMEM((messages, SLOTS, FB, NY), f32),
            pltpu.VMEM((messages, SLOTS, FB, NY), f32),
            pltpu.VMEM((messages, SLOTS, FB, NY), f32),
            pltpu.VMEM((messages, SLOTS, FB, NY), f32),
            pltpu.VMEM((2, 2, 8, NY), jnp.int32),
            pltpu.VMEM((2, 2, 8, NY), jnp.int32),
            pltpu.VMEM((RB + 1, nfreq, NY), f32),
            pltpu.VMEM((RB, nfreq, NY), f32),
            pltpu.VMEM((RB, nfreq, NY), f32),
            pltpu.VMEM((RB, nfreq, NY), f32),
            pltpu.VMEM((RB, 8, NY), f32),
            pltpu.VMEM((2, 8, points), f32),
            pltpu.VMEM((8, points), f32),
            dma((8,)),
            dma((RB,)),
            dma((blocks,)),
            dma((messages,)),
            dma((messages,)),
            dma((messages,)),
            dma((messages,)),
            dma((4,)),
            dma((4,)),
            dma((4,)),
            dma((4,)),
            dma((2,)),
            dma((2,)),
        ],
        compiler_params=pltpu.CompilerParams(
            collective_id=0, has_side_effects=True, vmem_limit_bytes=48 * 1024 * 1024
        ),
    )(
        *[
            pltpu.with_memory_space_constraint(operand, pltpu.HBM)
            for operand in (
                spectrum,
                wind_field,
                coupling,
                growth,
                dissipation,
                group_speed,
                refraction,
                depths,
                sea_mask,
                depth_index,
            )
        ]
    )
    return pl.pallas_call(
        hand_on,
        out_shape=jax.ShapeDtypeStruct((components, points), f32),
        in_specs=[pl.BlockSpec(memory_space=pltpu.VMEM)],
        out_specs=hbm,
        scratch_shapes=[dma((RB, 1))],
    )(pltpu.with_memory_space_constraint(moved, pltpu.VMEM))


def solution(mesh):
    in_specs = (
        P(None, ("comp", "space")),
        P(None, ("comp", "space")),
        P(),
        P(),
        P(),
        P(),
        P(),
        P(),
        P("space", None),
        P("space", None),
    )
    out_specs = P(None, ("comp", "space"))
    body = functools.partial(per_device, mesh.shape["comp"], mesh.shape["space"])
    return jax.shard_map(body, mesh=mesh, in_specs=in_specs, out_specs=out_specs, check_vma=False)
```

```python
import functools

import jax
import jax.numpy as jnp
import numpy as np
from jax import lax
from jax.experimental import pallas as pl
from jax.experimental.pallas import tpu as pltpu
from jax.sharding import PartitionSpec as P

ND = 36
NQ = 9
SPARE = 40
RB = 4
NY = 128
SUBSTEPS = 3
FB = 8
SLOTS = 6 * NQ
LOW, HIGH = (0, 1), (2, 3)
LINE = 8
RIGHT_AT = (0, 2 * NQ, 3 * NQ, 4 * NQ, 6 * NQ)
LEFT_AT = (0, NQ, 3 * NQ, 5 * NQ, 6 * NQ)
MESH = pl.DeviceIdType.MESH


def direction_tables():
    angles = np.float32(2.0 * np.pi) * np.arange(ND, dtype=np.float32) / np.float32(ND)
    cosine = np.cos(angles.astype(np.float64)).astype(np.float32)
    sine = np.sin(angles.astype(np.float64)).astype(np.float32)
    half_cos = np.float32(0.5) * (cosine + np.roll(cosine, -1))
    half_sin = np.float32(0.5) * (sine + np.roll(sine, -1))
    return np.concatenate([cosine, sine, half_cos, half_sin])


def face_of(nu, base, diff, second):
    return nu * (base + (1.0 - nu) * (0.5 * diff - (nu * (1.0 / 6.0) + (1.0 / 6.0)) * second))


def kernel(
    nfreq,
    ncomp,
    nspace,
    spectrum,
    wind_hbm,
    coupling,
    growth_hbm,
    dissipation_hbm,
    group_speed_hbm,
    refraction_hbm,
    depths_hbm,
    sea_mask_hbm,
    depth_index_hbm,
    out,
    trig,
    growth,
    dissipation,
    depths,
    wind,
    group_speed,
    refraction,
    sea_mask,
    depth_index,
    spec_v,
    coup_v,
    spec_b,
    nonlin,
    energy,
    work,
    send_l,
    send_r,
    recv_l,
    recv_r,
    coast_out,
    coast_in,
    gx,
    gy,
    rx,
    ry,
    mask_v,
    wind_v,
    ratio_v,
    small_sem,
    load_sem,
    coup_sem,
    send_l_sem,
    send_r_sem,
    recv_l_sem,
    recv_r_sem,
    part_send_l_sem,
    part_send_r_sem,
    part_recv_l_sem,
    part_recv_r_sem,
    coast_send_sem,
    coast_recv_sem,
):
    blocks = nfreq // FB
    rows_b = FB * ND
    components = nfreq * ND
    c = lax.axis_index("comp")
    s = lax.axis_index("space")
    total = ncomp * nspace
    n = s * ncomp + c
    before = lax.rem(n + total - 1, total)
    after = lax.rem(n + 1, total)
    left = (lax.rem(before, ncomp), lax.div(before, ncomp))
    right = (lax.rem(after, ncomp), lax.div(after, ncomp))
    edge_l = jnp.where(n > 0, 1.0, 0.0).astype(jnp.float32)
    edge_r = jnp.where(n < total - 1, 1.0, 0.0).astype(jnp.float32)

    barrier = pltpu.get_barrier_semaphore()
    pl.semaphore_signal(barrier, inc=1, device_id=left, device_id_type=MESH)
    pl.semaphore_signal(barrier, inc=1, device_id=right, device_id_type=MESH)

    def lanes(r):
        return slice(r * NY, (r + 1) * NY)

    def spec_load(r):
        return pltpu.make_async_copy(
            spectrum.at[:, lanes(r)], spec_v.at[r, pl.ds(0, components)], load_sem.at[r]
        )

    own_tile = pl.ds(pl.multiple_of(lax.div(c * RB, 8) * 8, 8), 8)
    small_loads = [
        pltpu.make_async_copy(src, dst, small_sem.at[j])
        for j, (src, dst) in enumerate(
            (
                (sea_mask_hbm.at[own_tile], sea_mask),
                (depth_index_hbm.at[own_tile], depth_index),
                (wind_hbm, wind),
                (growth_hbm, growth),
                (dissipation_hbm, dissipation),
                (group_speed_hbm, group_speed),
                (refraction_hbm, refraction),
                (depths_hbm, depths),
            )
        )
    ]
    for load in small_loads:
        load.start()

    def coup_load(b):
        rows = pl.ds(pl.multiple_of(b * rows_b, rows_b), rows_b)
        return pltpu.make_async_copy(coupling.at[rows], coup_v.at[rows], coup_sem.at[b])

    coup_load(0).start()

    for at, value in enumerate(direction_tables()):
        trig[at] = jnp.float32(value)
    for load in small_loads:
        load.wait()

    def to_left(k):
        return pltpu.make_async_remote_copy(
            src_ref=send_l.at[k],
            dst_ref=recv_r.at[k],
            send_sem=send_l_sem.at[k],
            recv_sem=recv_r_sem.at[k],
            device_id=left,
            device_id_type=MESH,
        )

    def to_right(k):
        return pltpu.make_async_remote_copy(
            src_ref=send_r.at[k],
            dst_ref=recv_l.at[k],
            send_sem=send_r_sem.at[k],
            recv_sem=recv_l_sem.at[k],
            device_id=right,
            device_id_type=MESH,
        )

    wind_v[0] = jnp.broadcast_to(wind[0:1, :], (8, RB * NY))
    wind_v[1] = jnp.broadcast_to(wind[1:2, :], (8, RB * NY))

    def pack_right(q, i, k, rows):
        at = RIGHT_AT[q]
        if q in (0, 3):
            send_r[k, at + 2 * i] = rows[RB - 2]
            send_r[k, at + 2 * i + 1] = rows[RB - 1]
        else:
            send_r[k, at + i] = rows[RB - 1]

    def pack_left(q, i, k, rows):
        at = LEFT_AT[q]
        if q in (0, 3):
            send_l[k, at + i] = rows[0]
        else:
            send_l[k, at + 2 * i] = rows[0]
            send_l[k, at + 2 * i + 1] = rows[1]

    sub8 = lax.broadcasted_iota(jnp.int32, (FB, NY), 0)

    def by_freq(table, b):
        values = jnp.zeros((FB, NY), jnp.float32)
        for j in range(FB):
            values = jnp.where(sub8 == j, table[b * FB + j], values)
        return values

    last = SUBSTEPS * blocks - 1

    def left_part(q):
        tiles = pl.ds(LEFT_AT[q], LEFT_AT[q + 1] - LEFT_AT[q])
        return pltpu.make_async_remote_copy(
            src_ref=send_l.at[last, tiles],
            dst_ref=recv_r.at[last, tiles],
            send_sem=part_send_l_sem.at[q],
            recv_sem=part_recv_r_sem.at[q],
            device_id=left,
            device_id_type=MESH,
        )

    def right_part(q):
        tiles = pl.ds(RIGHT_AT[q], RIGHT_AT[q + 1] - RIGHT_AT[q])
        return pltpu.make_async_remote_copy(
            src_ref=send_r.at[last, tiles],
            dst_ref=recv_l.at[last, tiles],
            send_sem=part_send_r_sem.at[q],
            recv_sem=part_recv_l_sem.at[q],
            device_id=right,
            device_id_type=MESH,
        )

    def prepare(r):
        spec_load(r).wait()

        def cast_rows(i, acc):
            rows = pl.ds(pl.multiple_of(i * 64, 64), 64)
            block = spec_v[r, rows, :]
            spec_b[rows, lanes(r)] = block.astype(jnp.bfloat16)
            return acc + jnp.sum(block.reshape(8, 8, NY), axis=0)

        acc = lax.fori_loop(0, components // 64, cast_rows, jnp.zeros((8, NY), jnp.float32))
        average = jnp.sum(acc, axis=0, keepdims=True) * (1.0 / components)
        ratio_v[:, lanes(r)] = jnp.broadcast_to(average / (average + 1.0), (8, NY))

    def source(b, pair):
        rows = pl.ds(pl.multiple_of(b * rows_b, rows_b), rows_b)
        columns = slice(pair[0] * NY, (pair[-1] + 1) * NY)
        product = jnp.dot(coup_v[rows, :], spec_b[:, columns], preferred_element_type=jnp.float32)
        for at, r in enumerate(pair):
            nonlin[r, :rows_b] = product[:, lanes(at)]
        grow = by_freq(growth, b)
        damp = by_freq(dissipation, b)
        damps = {r: damp * ratio_v[:, lanes(r)] for r in pair}

        def directions(i, inner):
            for q in range(4):
                d = q * NQ + i
                cosine = trig[d]
                sine = trig[ND + d]
                made = {}
                for r in pair:
                    forcing = jnp.maximum(cosine * wind_v[0, :, lanes(r)] + sine * wind_v[1, :, lanes(r)], 0.0)
                    value = spec_v[r, pl.ds(b * rows_b + d, FB, stride=ND), :]
                    extra = nonlin[r, pl.ds(d, FB, stride=ND), :]
                    value = value + (grow * (forcing * forcing) - damps[r]) * value + 0.25 * extra
                    energy[b, d, r] = value
                    made[r] = value
                if pair == HIGH:
                    pack_right(q, i, b, made)
                else:
                    pack_left(q, i, b, made)
            return inner

        lax.fori_loop(0, NQ, directions, 0, unroll=3)

    def open_with(first, second):
        for r in first:
            spec_load(r).start()
        prepare(first[0])
        for r in second:
            spec_load(r).start()
        prepare(first[1])
        coup_load(0).wait()
        source(0, first)

    def go_on_with(first, second):
        send_of(first, 0).start()
        for r in second:
            prepare(r)
        for b in range(1, blocks):
            coup_load(b).start()
        source(0, second)
        send_of(second, 0).start()

        def others(b, carry):
            coup_load(b).wait()
            source(b, first)
            send_of(first, b).start()
            source(b, second)
            send_of(second, b).start()
            return carry

        lax.fori_loop(1, blocks, others, 0)

    def send_of(pair, k):
        return to_left(k) if pair == LOW else to_right(k)

    low_first = jnp.logical_and(lax.rem(c, 2) == 0, c < ncomp - LINE)
    pl.when(low_first)(lambda: open_with(LOW, HIGH))
    pl.when(jnp.logical_not(low_first))(lambda: open_with(HIGH, LOW))

    row0 = lax.rem(c * RB, 8)
    own_mask = [sea_mask[pl.ds(row0 + r, 1), :] for r in range(RB)]
    own_index = [depth_index[pl.ds(row0 + r, 1), :] for r in range(RB)]
    for side, r in ((0, 0), (1, RB - 1)):
        coast_out[side, 0] = jnp.broadcast_to(own_mask[r], (8, NY))
        coast_out[side, 1] = jnp.broadcast_to(own_index[r], (8, NY))

    pl.semaphore_wait(barrier, 2)

    def coast_copy(side):
        return pltpu.make_async_remote_copy(
            src_ref=coast_out.at[side],
            dst_ref=coast_in.at[1 - side],
            send_sem=coast_send_sem.at[side],
            recv_sem=coast_recv_sem.at[1 - side],
            device_id=left if side == 0 else right,
            device_id_type=MESH,
        )

    for side in range(2):
        coast_copy(side).start()

    pl.when(low_first)(lambda: go_on_with(LOW, HIGH))
    pl.when(jnp.logical_not(low_first))(lambda: go_on_with(HIGH, LOW))

    for side in range(2):
        coast_copy(side).wait()
    mask_rows = (
        [coast_in[0, 0, 0:1, :].astype(jnp.float32) * edge_l]
        + [m.astype(jnp.float32) for m in own_mask]
        + [coast_in[1, 0, 0:1, :].astype(jnp.float32) * edge_r]
    )
    index_rows = [coast_in[0, 1, 0:1, :]] + own_index + [coast_in[1, 1, 0:1, :]]
    levels = depths.shape[0]
    level = lax.broadcasted_iota(jnp.int32, (levels, NY), 0)
    onehot = jnp.concatenate(
        [(jnp.broadcast_to(row, (levels, NY)) == level).astype(jnp.float32) for row in index_rows], axis=1
    )
    speeds = jnp.dot(
        group_speed[...], onehot, precision=lax.Precision.HIGHEST, preferred_element_type=jnp.float32
    )
    turning = jnp.dot(
        refraction[...],
        onehot[:, NY : (RB + 1) * NY],
        precision=lax.Precision.HIGHEST,
        preferred_element_type=jnp.float32,
    )
    lane_row = lax.broadcasted_iota(jnp.int32, (1, NY), 1)
    heights = []
    for row, mask in zip(index_rows, mask_rows):
        height = jnp.zeros((1, NY), jnp.float32)
        for entry in range(levels):
            height = jnp.where(row == entry, depths[entry], height)
        heights.append(height * mask)
    for j in range(RB + 1):
        pair = 0.5 * (speeds[:, lanes(j)] + speeds[:, lanes(j + 1)])
        gx[j] = pair * (mask_rows[j] * mask_rows[j + 1])
    for r in range(RB):
        mask = mask_rows[r + 1]
        own = speeds[:, lanes(r + 1)]
        beyond = jnp.where(lane_row == NY - 1, 0.0, pltpu.roll(jnp.broadcast_to(mask, (8, NY)), NY - 1, 1)[:1])
        gy[r] = 0.5 * (own + pltpu.roll(own, NY - 1, 1)) * (mask * beyond)
        wide = jnp.broadcast_to(heights[r + 1], (8, NY))
        up = jnp.where(lane_row == NY - 1, 0.0, pltpu.roll(wide, NY - 1, 1)[:1])
        down = jnp.where(lane_row == 0, 0.0, pltpu.roll(wide, 1, 1)[:1])
        rx[r] = turning[:, lanes(r)] * (0.5 * (heights[r + 2] - heights[r]))
        ry[r] = turning[:, lanes(r)] * (0.5 * (up - down))
        mask_v[r] = jnp.broadcast_to(mask, (8, NY))


    lane8 = lax.broadcasted_iota(jnp.int32, (FB, NY), 1)
    first_lane = lane8 == 0
    last_lanes = lane8 >= NY - 2

    def turn_face(freqs, d, r, base, diff, second, second_next):
        nu = trig[3 * ND + d] * rx[r, freqs, :] - trig[2 * ND + d] * ry[r, freqs, :]
        return face_of(nu, base, diff, jnp.where(nu >= 0.0, second, second_next))

    def last_passes(freqs, arrive, one_quadrant, emit):
        state = None
        cell = 2
        for q in range(4):
            arrive(q)
            one_quadrant(q)
            if q == 3:
                for d in range(4):
                    for r in range(RB):
                        work[ND + 1 + d, r] = work[1 + d, r]
            if q == 0:
                state = []
                for r in range(RB):
                    e0, e1, e2, e3 = (work[1 + d, r] for d in range(4))
                    d0, d1, d2 = e1 - e0, e2 - e1, e3 - e2
                    face = turn_face(freqs, 1, r, e1, d1, d1 - d0, d2 - d1)
                    state.append((e2, e3, d2, d2 - d1, face))
            until = (q + 1) * NQ - 2 if q < 3 else ND + 2
            while cell < until:
                made = []
                for r in range(RB):
                    e0, e1, diff, second, face_before = state[r]
                    e2 = work[cell + 3, r]
                    diff_next = e2 - e1
                    second_next = diff_next - diff
                    face = turn_face(freqs, cell % ND, r, e0, diff, second, second_next)
                    made.append((e0 - (face - face_before)) * mask_v[r])
                    state[r] = (e1, e2, diff_next, second_next, face)
                emit(None, None, cell % ND, made)
                cell += 1

    def passes(k, b, emit, arrive=None):
        if arrive is None:
            to_left(k).wait_recv()
            to_right(k).wait_recv()
        freqs = pl.ds(pl.multiple_of(b * FB, FB), FB)

        def x_and_y(q, i):
            d = q * NQ + i
            cosine = trig[d]
            sine = trig[ND + d]
            own = [energy[b, d, r] for r in range(RB)]
            low, high = RIGHT_AT[q], LEFT_AT[q]
            if q in (0, 3):
                ext = [recv_l[k, low + 2 * i] * edge_l, recv_l[k, low + 2 * i + 1] * edge_l]
                ext = ext + own + [recv_r[k, high + i] * edge_r]
                shift = 1
            else:
                ext = [recv_l[k, low + i] * edge_l] + own
                ext = ext + [recv_r[k, high + 2 * i] * edge_r, recv_r[k, high + 2 * i + 1] * edge_r]
                shift = 0
            diff = [ext[j + 1] - ext[j] for j in range(RB + 2)]
            second = [diff[j + 1] - diff[j] for j in range(RB + 1)]
            faces = []
            for j in range(RB + 1):
                nu = cosine * gx[j, freqs, :]
                faces.append(face_of(nu, ext[j + shift], diff[j + shift], second[j]))
            for r in range(RB):
                value = own[r] - (faces[r + 1] - faces[r])
                nu = sine * gy[r, freqs, :]
                if q in (0, 1):
                    behind = value - jnp.where(first_lane, 0.0, pltpu.roll(value, 1, 1))
                    ahead = pltpu.roll(value, NY - 1, 1) - value
                    face = face_of(nu, value, ahead, ahead - behind)
                else:
                    next1 = pltpu.roll(value, NY - 1, 1)
                    next2 = jnp.where(last_lanes, 0.0, pltpu.roll(value, NY - 2, 1))
                    ahead = next1 - value
                    face = face_of(nu, value, ahead, next2 - next1 - ahead)
                work[d + 1, r] = value - (face - pltpu.roll(face, 1, 1))

        def along_x_and_y(i, carry):
            for q in range(4):
                x_and_y(q, i)
            return carry

        def one_quadrant(q):
            def run(i, carry):
                x_and_y(q, i)
                return carry

            lax.fori_loop(0, NQ, run, 0, unroll=NQ)

        if arrive is not None:
            last_passes(freqs, arrive, one_quadrant, emit)
            return
        lax.fori_loop(0, NQ, along_x_and_y, 0, unroll=3)
        for r in range(RB):
            work[0, r] = work[ND, r]
            work[ND + 1, r] = work[1, r]
            work[ND + 2, r] = work[2, r]

        carry = []
        for r in range(RB):
            e34, e35, e0, e1 = work[ND - 1, r], work[ND, r], work[1, r], work[2, r]
            d34, d35, d0 = e35 - e34, e0 - e35, e1 - e0
            face = turn_face(freqs, ND - 1, r, e35, d35, d35 - d34, d0 - d35)
            carry.append((e0, e1, d0, d0 - d35, face))
        carry = tuple(carry)
        for q in range(4):

            def along_directions(i, state, q=q):
                d = q * NQ + i
                made = []
                later = []
                for r in range(RB):
                    e0, e1, diff, second, face_before = state[r]
                    e2 = work[d + 3, r]
                    diff_next = e2 - e1
                    second_next = diff_next - diff
                    face = turn_face(freqs, d, r, e0, diff, second, second_next)
                    made.append((e0 - (face - face_before)) * mask_v[r])
                    later.append((e1, e2, diff_next, second_next, face))
                emit(q, i, d, made)
                return tuple(later)

            carry = lax.fori_loop(0, NQ, along_directions, carry, unroll=3)

    def middle(k, carry):
        b = lax.rem(k, blocks)

        def emit(q, i, d, rows):
            for r in range(RB):
                energy[b, d, r] = rows[r]
            pack_right(q, i, k + blocks, rows)
            pack_left(q, i, k + blocks, rows)

        passes(k, b, emit)

        @pl.when(k + blocks < last)
        def _():
            to_right(k + blocks).start()
            to_left(k + blocks).start()

        @pl.when(k + blocks == last)
        def _():
            for q in range(4):
                right_part(q).start()
                left_part(q).start()

        return carry

    lax.fori_loop(0, (SUBSTEPS - 1) * blocks, middle, 0)

    def emit_out(b):
        def emit(q, i, d, rows):
            for r in range(RB):
                out[r, pl.ds(b * rows_b + d, FB, stride=ND), :] = rows[r]

        return emit

    def final(b, carry):
        passes(b + (SUBSTEPS - 1) * blocks, b, emit_out(b))
        return carry

    def arrive(q):
        left_part(q).wait_recv()
        right_part(q).wait_recv()

    lax.fori_loop(0, blocks - 1, final, 0)
    passes(last, blocks - 1, emit_out(blocks - 1), arrive)

    def drain(k, carry):
        to_left(k).wait_send()
        to_right(k).wait_send()
        return carry

    lax.fori_loop(0, last, drain, 0)
    for q in range(4):
        left_part(q).wait_send()
        right_part(q).wait_send()


def hand_on(moved, out, sems):
    chunks = sems.shape[1]
    rows = out.shape[0] // chunks
    copies = [
        pltpu.make_async_copy(
            moved.at[r, pl.ds(j * rows, rows)],
            out.at[pl.ds(j * rows, rows), r * NY : (r + 1) * NY],
            sems.at[r, j],
        )
        for r in range(RB)
        for j in range(chunks)
    ]
    for copy in copies:
        copy.start()
    for copy in copies:
        copy.wait()


def per_device(
    ncomp,
    nspace,
    spectrum,
    wind_field,
    coupling,
    growth,
    dissipation,
    group_speed,
    refraction,
    depths,
    sea_mask,
    depth_index,
):
    nfreq = growth.shape[0]
    blocks = nfreq // FB
    messages = SUBSTEPS * blocks
    components, points = spectrum.shape
    f32 = jnp.float32
    hbm = pl.BlockSpec(memory_space=pl.ANY)
    dma = pltpu.SemaphoreType.DMA
    moved = pl.pallas_call(
        functools.partial(kernel, nfreq, ncomp, nspace),
        out_shape=pltpu.VMEM((RB, components + SPARE, NY), f32),
        in_specs=[hbm] * 10,
        out_specs=pl.BlockSpec(memory_space=pltpu.VMEM),
        scratch_shapes=[
            pltpu.SMEM((4 * ND,), f32),
            pltpu.SMEM(growth.shape, f32),
            pltpu.SMEM(dissipation.shape, f32),
            pltpu.SMEM(depths.shape, f32),
            pltpu.VMEM(wind_field.shape, f32),
            pltpu.VMEM(group_speed.shape, f32),
            pltpu.VMEM(refraction.shape, f32),
            pltpu.VMEM((8, NY), jnp.int32),
            pltpu.VMEM((8, NY), jnp.int32),
            pltpu.VMEM((RB, components + SPARE, NY), f32),
            pltpu.VMEM((components, components), jnp.bfloat16),
            pltpu.VMEM((components, points), jnp.bfloat16),
            pltpu.VMEM((RB, FB * ND + SPARE, NY), f32),
            pltpu.VMEM((blocks, ND, RB, FB, NY), f32),
            pltpu.VMEM((ND + 5, RB, FB, NY), f32),
            pltpu.VMEM((messages, SLOTS, FB, NY), f32),
            pltpu.VMEM((messages, SLOTS, FB, NY), f32),
            pltpu.VMEM((messages, SLOTS, FB, NY), f32),
            pltpu.VMEM((messages, SLOTS, FB, NY), f32),
            pltpu.VMEM((2, 2, 8, NY), jnp.int32),
            pltpu.VMEM((2, 2, 8, NY), jnp.int32),
            pltpu.VMEM((RB + 1, nfreq, NY), f32),
            pltpu.VMEM((RB, nfreq, NY), f32),
            pltpu.VMEM((RB, nfreq, NY), f32),
            pltpu.VMEM((RB, nfreq, NY), f32),
            pltpu.VMEM((RB, 8, NY), f32),
            pltpu.VMEM((2, 8, points), f32),
            pltpu.VMEM((8, points), f32),
            dma((8,)),
            dma((RB,)),
            dma((blocks,)),
            dma((messages,)),
            dma((messages,)),
            dma((messages,)),
            dma((messages,)),
            dma((4,)),
            dma((4,)),
            dma((4,)),
            dma((4,)),
            dma((2,)),
            dma((2,)),
        ],
        compiler_params=pltpu.CompilerParams(
            collective_id=0, has_side_effects=True, vmem_limit_bytes=48 * 1024 * 1024
        ),
    )(
        *[
            pltpu.with_memory_space_constraint(operand, pltpu.HBM)
            for operand in (
                spectrum,
                wind_field,
                coupling,
                growth,
                dissipation,
                group_speed,
                refraction,
                depths,
                sea_mask,
                depth_index,
            )
        ]
    )
    return pl.pallas_call(
        hand_on,
        out_shape=jax.ShapeDtypeStruct((components, points), f32),
        in_specs=[pl.BlockSpec(memory_space=pltpu.VMEM)],
        out_specs=hbm,
        scratch_shapes=[dma((RB, 1))],
    )(pltpu.with_memory_space_constraint(moved, pltpu.VMEM))


def solution(mesh):
    in_specs = (
        P(None, ("comp", "space")),
        P(None, ("comp", "space")),
        P(),
        P(),
        P(),
        P(),
        P(),
        P(),
        P("space", None),
        P("space", None),
    )
    out_specs = P(None, ("comp", "space"))
    body = functools.partial(per_device, mesh.shape["comp"], mesh.shape["space"])
    return jax.shard_map(body, mesh=mesh, in_specs=in_specs, out_specs=out_specs, check_vma=False)
```

```python
import functools

import jax
import jax.numpy as jnp
import numpy as np
from jax import lax
from jax.experimental import pallas as pl
from jax.experimental.pallas import tpu as pltpu
from jax.sharding import PartitionSpec as P

ND = 36
NQ = 9
SPARE = 40
RB = 4
NY = 128
SUBSTEPS = 3
FB = 8
SLOTS = 6 * NQ
LOW, HIGH = (0, 1), (2, 3)
LINE = 8
RIGHT_AT = (0, 2 * NQ, 3 * NQ, 4 * NQ, 6 * NQ)
LEFT_AT = (0, NQ, 3 * NQ, 5 * NQ, 6 * NQ)
MESH = pl.DeviceIdType.MESH


def direction_tables():
    angles = np.float32(2.0 * np.pi) * np.arange(ND, dtype=np.float32) / np.float32(ND)
    cosine = np.cos(angles.astype(np.float64)).astype(np.float32)
    sine = np.sin(angles.astype(np.float64)).astype(np.float32)
    half_cos = np.float32(0.5) * (cosine + np.roll(cosine, -1))
    half_sin = np.float32(0.5) * (sine + np.roll(sine, -1))
    return np.concatenate([cosine, sine, half_cos, half_sin])


def face_of(nu, base, diff, second):
    return nu * (base + (1.0 - nu) * (0.5 * diff - (nu * (1.0 / 6.0) + (1.0 / 6.0)) * second))


def kernel(
    nfreq,
    ncomp,
    nspace,
    spectrum,
    wind_hbm,
    coupling,
    growth_hbm,
    dissipation_hbm,
    group_speed_hbm,
    refraction_hbm,
    depths_hbm,
    sea_mask_hbm,
    depth_index_hbm,
    out,
    trig,
    growth,
    dissipation,
    depths,
    wind,
    group_speed,
    refraction,
    sea_mask,
    depth_index,
    spec_v,
    coup_v,
    spec_b,
    nonlin,
    energy,
    work,
    send_l,
    send_r,
    recv_l,
    recv_r,
    coast_out,
    coast_in,
    gx,
    gy,
    rx,
    ry,
    mask_v,
    wind_v,
    ratio_v,
    small_sem,
    load_sem,
    coup_sem,
    send_l_sem,
    send_r_sem,
    recv_l_sem,
    recv_r_sem,
    part_send_l_sem,
    part_send_r_sem,
    part_recv_l_sem,
    part_recv_r_sem,
    coast_send_sem,
    coast_recv_sem,
):
    blocks = nfreq // FB
    rows_b = FB * ND
    components = nfreq * ND
    c = lax.axis_index("comp")
    s = lax.axis_index("space")
    total = ncomp * nspace
    n = s * ncomp + c
    before = lax.rem(n + total - 1, total)
    after = lax.rem(n + 1, total)
    left = (lax.rem(before, ncomp), lax.div(before, ncomp))
    right = (lax.rem(after, ncomp), lax.div(after, ncomp))
    edge_l = jnp.where(n > 0, 1.0, 0.0).astype(jnp.float32)
    edge_r = jnp.where(n < total - 1, 1.0, 0.0).astype(jnp.float32)

    barrier = pltpu.get_barrier_semaphore()
    pl.semaphore_signal(barrier, inc=1, device_id=left, device_id_type=MESH)
    pl.semaphore_signal(barrier, inc=1, device_id=right, device_id_type=MESH)

    def lanes(r):
        return slice(r * NY, (r + 1) * NY)

    def spec_load(r):
        return pltpu.make_async_copy(
            spectrum.at[:, lanes(r)], spec_v.at[r, pl.ds(0, components)], load_sem.at[r]
        )

    own_tile = pl.ds(pl.multiple_of(lax.div(c * RB, 8) * 8, 8), 8)
    small_loads = [
        pltpu.make_async_copy(src, dst, small_sem.at[j])
        for j, (src, dst) in enumerate(
            (
                (sea_mask_hbm.at[own_tile], sea_mask),
                (depth_index_hbm.at[own_tile], depth_index),
                (wind_hbm, wind),
                (growth_hbm, growth),
                (dissipation_hbm, dissipation),
                (group_speed_hbm, group_speed),
                (refraction_hbm, refraction),
                (depths_hbm, depths),
            )
        )
    ]
    for load in small_loads:
        load.start()

    def coup_load(b):
        rows = pl.ds(pl.multiple_of(b * rows_b, rows_b), rows_b)
        return pltpu.make_async_copy(coupling.at[rows], coup_v.at[rows], coup_sem.at[b])


    for at, value in enumerate(direction_tables()):
        trig[at] = jnp.float32(value)
    for load in small_loads:
        load.wait()

    def to_left(k):
        return pltpu.make_async_remote_copy(
            src_ref=send_l.at[k],
            dst_ref=recv_r.at[k],
            send_sem=send_l_sem.at[k],
            recv_sem=recv_r_sem.at[k],
            device_id=left,
            device_id_type=MESH,
        )

    def to_right(k):
        return pltpu.make_async_remote_copy(
            src_ref=send_r.at[k],
            dst_ref=recv_l.at[k],
            send_sem=send_r_sem.at[k],
            recv_sem=recv_l_sem.at[k],
            device_id=right,
            device_id_type=MESH,
        )

    wind_v[0] = jnp.broadcast_to(wind[0:1, :], (8, RB * NY))
    wind_v[1] = jnp.broadcast_to(wind[1:2, :], (8, RB * NY))

    def pack_right(q, i, k, rows):
        at = RIGHT_AT[q]
        if q in (0, 3):
            send_r[k, at + 2 * i] = rows[RB - 2]
            send_r[k, at + 2 * i + 1] = rows[RB - 1]
        else:
            send_r[k, at + i] = rows[RB - 1]

    def pack_left(q, i, k, rows):
        at = LEFT_AT[q]
        if q in (0, 3):
            send_l[k, at + i] = rows[0]
        else:
            send_l[k, at + 2 * i] = rows[0]
            send_l[k, at + 2 * i + 1] = rows[1]

    sub8 = lax.broadcasted_iota(jnp.int32, (FB, NY), 0)

    def by_freq(table, b):
        values = jnp.zeros((FB, NY), jnp.float32)
        for j in range(FB):
            values = jnp.where(sub8 == j, table[b * FB + j], values)
        return values

    last = SUBSTEPS * blocks - 1

    def left_part(q):
        tiles = pl.ds(LEFT_AT[q], LEFT_AT[q + 1] - LEFT_AT[q])
        return pltpu.make_async_remote_copy(
            src_ref=send_l.at[last, tiles],
            dst_ref=recv_r.at[last, tiles],
            send_sem=part_send_l_sem.at[q],
            recv_sem=part_recv_r_sem.at[q],
            device_id=left,
            device_id_type=MESH,
        )

    def right_part(q):
        tiles = pl.ds(RIGHT_AT[q], RIGHT_AT[q + 1] - RIGHT_AT[q])
        return pltpu.make_async_remote_copy(
            src_ref=send_r.at[last, tiles],
            dst_ref=recv_l.at[last, tiles],
            send_sem=part_send_r_sem.at[q],
            recv_sem=part_recv_l_sem.at[q],
            device_id=right,
            device_id_type=MESH,
        )

    def prepare(r):
        spec_load(r).wait()

        def cast_rows(i, acc):
            rows = pl.ds(pl.multiple_of(i * 64, 64), 64)
            block = spec_v[r, rows, :]
            spec_b[rows, lanes(r)] = block.astype(jnp.bfloat16)
            return acc + jnp.sum(block.reshape(8, 8, NY), axis=0)

        acc = lax.fori_loop(0, components // 64, cast_rows, jnp.zeros((8, NY), jnp.float32))
        average = jnp.sum(acc, axis=0, keepdims=True) * (1.0 / components)
        ratio_v[:, lanes(r)] = jnp.broadcast_to(average / (average + 1.0), (8, NY))

    def source(b, pair):
        rows = pl.ds(pl.multiple_of(b * rows_b, rows_b), rows_b)
        columns = slice(pair[0] * NY, (pair[-1] + 1) * NY)
        product = jnp.dot(coup_v[rows, :], spec_b[:, columns], preferred_element_type=jnp.float32)
        for at, r in enumerate(pair):
            nonlin[r, :rows_b] = product[:, lanes(at)]
        grow = by_freq(growth, b)
        damp = by_freq(dissipation, b)
        damps = {r: damp * ratio_v[:, lanes(r)] for r in pair}

        def directions(i, inner):
            for q in range(4):
                d = q * NQ + i
                cosine = trig[d]
                sine = trig[ND + d]
                made = {}
                for r in pair:
                    forcing = jnp.maximum(cosine * wind_v[0, :, lanes(r)] + sine * wind_v[1, :, lanes(r)], 0.0)
                    value = spec_v[r, pl.ds(b * rows_b + d, FB, stride=ND), :]
                    extra = nonlin[r, pl.ds(d, FB, stride=ND), :]
                    value = value + (grow * (forcing * forcing) - damps[r]) * value + 0.25 * extra
                    energy[b, d, r] = value
                    made[r] = value
                if pair == HIGH:
                    pack_right(q, i, b, made)
                else:
                    pack_left(q, i, b, made)
            return inner

        lax.fori_loop(0, NQ, directions, 0, unroll=3)

    def open_with(first, second):
        for r in first:
            spec_load(r).start()
        coup_load(0).start()
        prepare(first[0])
        prepare(first[1])
        coup_load(0).wait()
        for r in second:
            spec_load(r).start()
        source(0, first)

    def go_on_with(first, second):
        send_of(first, 0).start()
        for r in second:
            prepare(r)
        for b in range(1, blocks):
            coup_load(b).start()
        source(0, second)
        send_of(second, 0).start()

        def others(b, carry):
            coup_load(b).wait()
            source(b, first)
            send_of(first, b).start()
            source(b, second)
            send_of(second, b).start()
            return carry

        lax.fori_loop(1, blocks, others, 0)

    def send_of(pair, k):
        return to_left(k) if pair == LOW else to_right(k)

    low_first = jnp.logical_and(lax.rem(c, 2) == 0, c < ncomp - LINE)
    pl.when(low_first)(lambda: open_with(LOW, HIGH))
    pl.when(jnp.logical_not(low_first))(lambda: open_with(HIGH, LOW))

    row0 = lax.rem(c * RB, 8)
    own_mask = [sea_mask[pl.ds(row0 + r, 1), :] for r in range(RB)]
    own_index = [depth_index[pl.ds(row0 + r, 1), :] for r in range(RB)]
    for side, r in ((0, 0), (1, RB - 1)):
        coast_out[side, 0] = jnp.broadcast_to(own_mask[r], (8, NY))
        coast_out[side, 1] = jnp.broadcast_to(own_index[r], (8, NY))

    pl.semaphore_wait(barrier, 2)

    def coast_copy(side):
        return pltpu.make_async_remote_copy(
            src_ref=coast_out.at[side],
            dst_ref=coast_in.at[1 - side],
            send_sem=coast_send_sem.at[side],
            recv_sem=coast_recv_sem.at[1 - side],
            device_id=left if side == 0 else right,
            device_id_type=MESH,
        )

    for side in range(2):
        coast_copy(side).start()

    pl.when(low_first)(lambda: go_on_with(LOW, HIGH))
    pl.when(jnp.logical_not(low_first))(lambda: go_on_with(HIGH, LOW))

    for side in range(2):
        coast_copy(side).wait()
    mask_rows = (
        [coast_in[0, 0, 0:1, :].astype(jnp.float32) * edge_l]
        + [m.astype(jnp.float32) for m in own_mask]
        + [coast_in[1, 0, 0:1, :].astype(jnp.float32) * edge_r]
    )
    index_rows = [coast_in[0, 1, 0:1, :]] + own_index + [coast_in[1, 1, 0:1, :]]
    levels = depths.shape[0]
    level = lax.broadcasted_iota(jnp.int32, (levels, NY), 0)
    onehot = jnp.concatenate(
        [(jnp.broadcast_to(row, (levels, NY)) == level).astype(jnp.float32) for row in index_rows], axis=1
    )
    speeds = jnp.dot(
        group_speed[...], onehot, precision=lax.Precision.HIGHEST, preferred_element_type=jnp.float32
    )
    turning = jnp.dot(
        refraction[...],
        onehot[:, NY : (RB + 1) * NY],
        precision=lax.Precision.HIGHEST,
        preferred_element_type=jnp.float32,
    )
    lane_row = lax.broadcasted_iota(jnp.int32, (1, NY), 1)
    heights = []
    for row, mask in zip(index_rows, mask_rows):
        height = jnp.zeros((1, NY), jnp.float32)
        for entry in range(levels):
            height = jnp.where(row == entry, depths[entry], height)
        heights.append(height * mask)
    for j in range(RB + 1):
        pair = 0.5 * (speeds[:, lanes(j)] + speeds[:, lanes(j + 1)])
        gx[j] = pair * (mask_rows[j] * mask_rows[j + 1])
    for r in range(RB):
        mask = mask_rows[r + 1]
        own = speeds[:, lanes(r + 1)]
        beyond = jnp.where(lane_row == NY - 1, 0.0, pltpu.roll(jnp.broadcast_to(mask, (8, NY)), NY - 1, 1)[:1])
        gy[r] = 0.5 * (own + pltpu.roll(own, NY - 1, 1)) * (mask * beyond)
        wide = jnp.broadcast_to(heights[r + 1], (8, NY))
        up = jnp.where(lane_row == NY - 1, 0.0, pltpu.roll(wide, NY - 1, 1)[:1])
        down = jnp.where(lane_row == 0, 0.0, pltpu.roll(wide, 1, 1)[:1])
        rx[r] = turning[:, lanes(r)] * (0.5 * (heights[r + 2] - heights[r]))
        ry[r] = turning[:, lanes(r)] * (0.5 * (up - down))
        mask_v[r] = jnp.broadcast_to(mask, (8, NY))


    lane8 = lax.broadcasted_iota(jnp.int32, (FB, NY), 1)
    first_lane = lane8 == 0
    last_lanes = lane8 >= NY - 2

    def turn_face(freqs, d, r, base, diff, second, second_next):
        nu = trig[3 * ND + d] * rx[r, freqs, :] - trig[2 * ND + d] * ry[r, freqs, :]
        return face_of(nu, base, diff, jnp.where(nu >= 0.0, second, second_next))

    def last_passes(freqs, arrive, one_quadrant, emit):
        state = None
        cell = 2
        for q in range(4):
            arrive(q)
            one_quadrant(q)
            if q == 3:
                for d in range(4):
                    for r in range(RB):
                        work[ND + 1 + d, r] = work[1 + d, r]
            if q == 0:
                state = []
                for r in range(RB):
                    e0, e1, e2, e3 = (work[1 + d, r] for d in range(4))
                    d0, d1, d2 = e1 - e0, e2 - e1, e3 - e2
                    face = turn_face(freqs, 1, r, e1, d1, d1 - d0, d2 - d1)
                    state.append((e2, e3, d2, d2 - d1, face))
            until = (q + 1) * NQ - 2 if q < 3 else ND + 2
            while cell < until:
                made = []
                for r in range(RB):
                    e0, e1, diff, second, face_before = state[r]
                    e2 = work[cell + 3, r]
                    diff_next = e2 - e1
                    second_next = diff_next - diff
                    face = turn_face(freqs, cell % ND, r, e0, diff, second, second_next)
                    made.append((e0 - (face - face_before)) * mask_v[r])
                    state[r] = (e1, e2, diff_next, second_next, face)
                emit(None, None, cell % ND, made)
                cell += 1

    def passes(k, b, emit, arrive=None):
        if arrive is None:
            to_left(k).wait_recv()
            to_right(k).wait_recv()
        freqs = pl.ds(pl.multiple_of(b * FB, FB), FB)

        def x_and_y(q, i):
            d = q * NQ + i
            cosine = trig[d]
            sine = trig[ND + d]
            own = [energy[b, d, r] for r in range(RB)]
            low, high = RIGHT_AT[q], LEFT_AT[q]
            if q in (0, 3):
                ext = [recv_l[k, low + 2 * i] * edge_l, recv_l[k, low + 2 * i + 1] * edge_l]
                ext = ext + own + [recv_r[k, high + i] * edge_r]
                shift = 1
            else:
                ext = [recv_l[k, low + i] * edge_l] + own
                ext = ext + [recv_r[k, high + 2 * i] * edge_r, recv_r[k, high + 2 * i + 1] * edge_r]
                shift = 0
            diff = [ext[j + 1] - ext[j] for j in range(RB + 2)]
            second = [diff[j + 1] - diff[j] for j in range(RB + 1)]
            faces = []
            for j in range(RB + 1):
                nu = cosine * gx[j, freqs, :]
                faces.append(face_of(nu, ext[j + shift], diff[j + shift], second[j]))
            for r in range(RB):
                value = own[r] - (faces[r + 1] - faces[r])
                nu = sine * gy[r, freqs, :]
                if q in (0, 1):
                    behind = value - jnp.where(first_lane, 0.0, pltpu.roll(value, 1, 1))
                    ahead = pltpu.roll(value, NY - 1, 1) - value
                    face = face_of(nu, value, ahead, ahead - behind)
                else:
                    next1 = pltpu.roll(value, NY - 1, 1)
                    next2 = jnp.where(last_lanes, 0.0, pltpu.roll(value, NY - 2, 1))
                    ahead = next1 - value
                    face = face_of(nu, value, ahead, next2 - next1 - ahead)
                work[d + 1, r] = value - (face - pltpu.roll(face, 1, 1))

        def along_x_and_y(i, carry):
            for q in range(4):
                x_and_y(q, i)
            return carry

        def one_quadrant(q):
            def run(i, carry):
                x_and_y(q, i)
                return carry

            lax.fori_loop(0, NQ, run, 0, unroll=NQ)

        if arrive is not None:
            last_passes(freqs, arrive, one_quadrant, emit)
            return
        lax.fori_loop(0, NQ, along_x_and_y, 0, unroll=3)
        for r in range(RB):
            work[0, r] = work[ND, r]
            work[ND + 1, r] = work[1, r]
            work[ND + 2, r] = work[2, r]

        carry = []
        for r in range(RB):
            e34, e35, e0, e1 = work[ND - 1, r], work[ND, r], work[1, r], work[2, r]
            d34, d35, d0 = e35 - e34, e0 - e35, e1 - e0
            face = turn_face(freqs, ND - 1, r, e35, d35, d35 - d34, d0 - d35)
            carry.append((e0, e1, d0, d0 - d35, face))
        carry = tuple(carry)
        for q in range(4):

            def along_directions(i, state, q=q):
                d = q * NQ + i
                made = []
                later = []
                for r in range(RB):
                    e0, e1, diff, second, face_before = state[r]
                    e2 = work[d + 3, r]
                    diff_next = e2 - e1
                    second_next = diff_next - diff
                    face = turn_face(freqs, d, r, e0, diff, second, second_next)
                    made.append((e0 - (face - face_before)) * mask_v[r])
                    later.append((e1, e2, diff_next, second_next, face))
                emit(q, i, d, made)
                return tuple(later)

            carry = lax.fori_loop(0, NQ, along_directions, carry, unroll=3)

    def middle(k, carry):
        b = lax.rem(k, blocks)

        def emit(q, i, d, rows):
            for r in range(RB):
                energy[b, d, r] = rows[r]
            pack_right(q, i, k + blocks, rows)
            pack_left(q, i, k + blocks, rows)

        passes(k, b, emit)

        @pl.when(jnp.logical_and(k + blocks < last, lax.rem(c, 2) == 0))
        def _():
            to_right(k + blocks).start()
            to_left(k + blocks).start()

        @pl.when(jnp.logical_and(k + blocks < last, lax.rem(c, 2) == 1))
        def _():
            to_left(k + blocks).start()
            to_right(k + blocks).start()

        @pl.when(k + blocks == last)
        def _():
            for q in range(4):
                right_part(q).start()
                left_part(q).start()

        return carry

    lax.fori_loop(0, (SUBSTEPS - 1) * blocks, middle, 0)

    def emit_out(b):
        def emit(q, i, d, rows):
            for r in range(RB):
                out[r, pl.ds(b * rows_b + d, FB, stride=ND), :] = rows[r]

        return emit

    def final(b, carry):
        passes(b + (SUBSTEPS - 1) * blocks, b, emit_out(b))
        return carry

    def arrive(q):
        left_part(q).wait_recv()
        right_part(q).wait_recv()

    lax.fori_loop(0, blocks - 1, final, 0)
    passes(last, blocks - 1, emit_out(blocks - 1), arrive)

    def drain(k, carry):
        to_left(k).wait_send()
        to_right(k).wait_send()
        return carry

    lax.fori_loop(0, last, drain, 0)
    for q in range(4):
        left_part(q).wait_send()
        right_part(q).wait_send()


def hand_on(moved, out, sems):
    chunks = sems.shape[1]
    rows = out.shape[0] // chunks
    copies = [
        pltpu.make_async_copy(
            moved.at[r, pl.ds(j * rows, rows)],
            out.at[pl.ds(j * rows, rows), r * NY : (r + 1) * NY],
            sems.at[r, j],
        )
        for r in range(RB)
        for j in range(chunks)
    ]
    for copy in copies:
        copy.start()
    for copy in copies:
        copy.wait()


def per_device(
    ncomp,
    nspace,
    spectrum,
    wind_field,
    coupling,
    growth,
    dissipation,
    group_speed,
    refraction,
    depths,
    sea_mask,
    depth_index,
):
    nfreq = growth.shape[0]
    blocks = nfreq // FB
    messages = SUBSTEPS * blocks
    components, points = spectrum.shape
    f32 = jnp.float32
    hbm = pl.BlockSpec(memory_space=pl.ANY)
    dma = pltpu.SemaphoreType.DMA
    moved = pl.pallas_call(
        functools.partial(kernel, nfreq, ncomp, nspace),
        out_shape=pltpu.VMEM((RB, components + SPARE, NY), f32),
        in_specs=[hbm] * 10,
        out_specs=pl.BlockSpec(memory_space=pltpu.VMEM),
        scratch_shapes=[
            pltpu.SMEM((4 * ND,), f32),
            pltpu.SMEM(growth.shape, f32),
            pltpu.SMEM(dissipation.shape, f32),
            pltpu.SMEM(depths.shape, f32),
            pltpu.VMEM(wind_field.shape, f32),
            pltpu.VMEM(group_speed.shape, f32),
            pltpu.VMEM(refraction.shape, f32),
            pltpu.VMEM((8, NY), jnp.int32),
            pltpu.VMEM((8, NY), jnp.int32),
            pltpu.VMEM((RB, components + SPARE, NY), f32),
            pltpu.VMEM((components, components), jnp.bfloat16),
            pltpu.VMEM((components, points), jnp.bfloat16),
            pltpu.VMEM((RB, FB * ND + SPARE, NY), f32),
            pltpu.VMEM((blocks, ND, RB, FB, NY), f32),
            pltpu.VMEM((ND + 5, RB, FB, NY), f32),
            pltpu.VMEM((messages, SLOTS, FB, NY), f32),
            pltpu.VMEM((messages, SLOTS, FB, NY), f32),
            pltpu.VMEM((messages, SLOTS, FB, NY), f32),
            pltpu.VMEM((messages, SLOTS, FB, NY), f32),
            pltpu.VMEM((2, 2, 8, NY), jnp.int32),
            pltpu.VMEM((2, 2, 8, NY), jnp.int32),
            pltpu.VMEM((RB + 1, nfreq, NY), f32),
            pltpu.VMEM((RB, nfreq, NY), f32),
            pltpu.VMEM((RB, nfreq, NY), f32),
            pltpu.VMEM((RB, nfreq, NY), f32),
            pltpu.VMEM((RB, 8, NY), f32),
            pltpu.VMEM((2, 8, points), f32),
            pltpu.VMEM((8, points), f32),
            dma((8,)),
            dma((RB,)),
            dma((blocks,)),
            dma((messages,)),
            dma((messages,)),
            dma((messages,)),
            dma((messages,)),
            dma((4,)),
            dma((4,)),
            dma((4,)),
            dma((4,)),
            dma((2,)),
            dma((2,)),
        ],
        compiler_params=pltpu.CompilerParams(
            collective_id=0, has_side_effects=True, vmem_limit_bytes=48 * 1024 * 1024
        ),
    )(
        *[
            pltpu.with_memory_space_constraint(operand, pltpu.HBM)
            for operand in (
                spectrum,
                wind_field,
                coupling,
                growth,
                dissipation,
                group_speed,
                refraction,
                depths,
                sea_mask,
                depth_index,
            )
        ]
    )
    return pl.pallas_call(
        hand_on,
        out_shape=jax.ShapeDtypeStruct((components, points), f32),
        in_specs=[pl.BlockSpec(memory_space=pltpu.VMEM)],
        out_specs=hbm,
        scratch_shapes=[dma((RB, 1))],
    )(pltpu.with_memory_space_constraint(moved, pltpu.VMEM))


def solution(mesh):
    in_specs = (
        P(None, ("comp", "space")),
        P(None, ("comp", "space")),
        P(),
        P(),
        P(),
        P(),
        P(),
        P(),
        P("space", None),
        P("space", None),
    )
    out_specs = P(None, ("comp", "space"))
    body = functools.partial(per_device, mesh.shape["comp"], mesh.shape["space"])
    return jax.shard_map(body, mesh=mesh, in_specs=in_specs, out_specs=out_specs, check_vma=False)
```

```python
import functools

import jax
import jax.numpy as jnp
import numpy as np
from jax import lax
from jax.experimental import pallas as pl
from jax.experimental.pallas import tpu as pltpu
from jax.sharding import PartitionSpec as P

ND = 36
NQ = 9
SPARE = 40
RB = 4
NY = 128
SUBSTEPS = 3
FB = 8
SLOTS = 6 * NQ
LOW, HIGH = (0, 1), (2, 3)
LINE = 8
RIGHT_AT = (0, 2 * NQ, 3 * NQ, 4 * NQ, 6 * NQ)
LEFT_AT = (0, NQ, 3 * NQ, 5 * NQ, 6 * NQ)
MESH = pl.DeviceIdType.MESH


def direction_tables():
    angles = np.float32(2.0 * np.pi) * np.arange(ND, dtype=np.float32) / np.float32(ND)
    cosine = np.cos(angles.astype(np.float64)).astype(np.float32)
    sine = np.sin(angles.astype(np.float64)).astype(np.float32)
    half_cos = np.float32(0.5) * (cosine + np.roll(cosine, -1))
    half_sin = np.float32(0.5) * (sine + np.roll(sine, -1))
    return np.concatenate([cosine, sine, half_cos, half_sin])


def face_of(nu, base, diff, second):
    return nu * (base + (1.0 - nu) * (0.5 * diff - (nu * (1.0 / 6.0) + (1.0 / 6.0)) * second))


def kernel(
    nfreq,
    ncomp,
    nspace,
    spectrum,
    wind_hbm,
    coupling,
    growth_hbm,
    dissipation_hbm,
    group_speed_hbm,
    refraction_hbm,
    depths_hbm,
    sea_mask_hbm,
    depth_index_hbm,
    out,
    trig,
    growth,
    dissipation,
    depths,
    wind,
    group_speed,
    refraction,
    sea_mask,
    depth_index,
    spec_v,
    coup_v,
    spec_b,
    nonlin,
    energy,
    work,
    send_l,
    send_r,
    recv_l,
    recv_r,
    coast_out,
    coast_in,
    gx,
    gy,
    rx,
    ry,
    mask_v,
    wind_v,
    ratio_v,
    small_sem,
    load_sem,
    coup_sem,
    send_l_sem,
    send_r_sem,
    recv_l_sem,
    recv_r_sem,
    part_send_l_sem,
    part_send_r_sem,
    part_recv_l_sem,
    part_recv_r_sem,
    coast_send_sem,
    coast_recv_sem,
):
    blocks = nfreq // FB
    rows_b = FB * ND
    components = nfreq * ND
    c = lax.axis_index("comp")
    s = lax.axis_index("space")
    total = ncomp * nspace
    n = s * ncomp + c
    before = lax.rem(n + total - 1, total)
    after = lax.rem(n + 1, total)
    left = (lax.rem(before, ncomp), lax.div(before, ncomp))
    right = (lax.rem(after, ncomp), lax.div(after, ncomp))
    edge_l = jnp.where(n > 0, 1.0, 0.0).astype(jnp.float32)
    edge_r = jnp.where(n < total - 1, 1.0, 0.0).astype(jnp.float32)

    barrier = pltpu.get_barrier_semaphore()
    pl.semaphore_signal(barrier, inc=1, device_id=left, device_id_type=MESH)
    pl.semaphore_signal(barrier, inc=1, device_id=right, device_id_type=MESH)

    def lanes(r):
        return slice(r * NY, (r + 1) * NY)

    def spec_load(r):
        return pltpu.make_async_copy(
            spectrum.at[:, lanes(r)], spec_v.at[r, pl.ds(0, components)], load_sem.at[r]
        )

    own_tile = pl.ds(pl.multiple_of(lax.div(c * RB, 8) * 8, 8), 8)
    small_loads = [
        pltpu.make_async_copy(src, dst, small_sem.at[j])
        for j, (src, dst) in enumerate(
            (
                (sea_mask_hbm.at[own_tile], sea_mask),
                (depth_index_hbm.at[own_tile], depth_index),
                (wind_hbm, wind),
                (growth_hbm, growth),
                (dissipation_hbm, dissipation),
                (group_speed_hbm, group_speed),
                (refraction_hbm, refraction),
                (depths_hbm, depths),
            )
        )
    ]
    for load in small_loads:
        load.start()

    def coup_load(b):
        rows = pl.ds(pl.multiple_of(b * rows_b, rows_b), rows_b)
        return pltpu.make_async_copy(coupling.at[rows], coup_v.at[rows], coup_sem.at[b])


    for at, value in enumerate(direction_tables()):
        trig[at] = jnp.float32(value)
    for load in small_loads:
        load.wait()

    def to_left(k):
        return pltpu.make_async_remote_copy(
            src_ref=send_l.at[k],
            dst_ref=recv_r.at[k],
            send_sem=send_l_sem.at[k],
            recv_sem=recv_r_sem.at[k],
            device_id=left,
            device_id_type=MESH,
        )

    def to_right(k):
        return pltpu.make_async_remote_copy(
            src_ref=send_r.at[k],
            dst_ref=recv_l.at[k],
            send_sem=send_r_sem.at[k],
            recv_sem=recv_l_sem.at[k],
            device_id=right,
            device_id_type=MESH,
        )

    wind_v[0] = jnp.broadcast_to(wind[0:1, :], (8, RB * NY))
    wind_v[1] = jnp.broadcast_to(wind[1:2, :], (8, RB * NY))

    def pack_right(q, i, k, rows):
        at = RIGHT_AT[q]
        if q in (0, 3):
            send_r[k, at + 2 * i] = rows[RB - 2]
            send_r[k, at + 2 * i + 1] = rows[RB - 1]
        else:
            send_r[k, at + i] = rows[RB - 1]

    def pack_left(q, i, k, rows):
        at = LEFT_AT[q]
        if q in (0, 3):
            send_l[k, at + i] = rows[0]
        else:
            send_l[k, at + 2 * i] = rows[0]
            send_l[k, at + 2 * i + 1] = rows[1]

    sub8 = lax.broadcasted_iota(jnp.int32, (FB, NY), 0)

    def by_freq(table, b):
        values = jnp.zeros((FB, NY), jnp.float32)
        for j in range(FB):
            values = jnp.where(sub8 == j, table[b * FB + j], values)
        return values

    last = SUBSTEPS * blocks - 1

    def left_part(q):
        tiles = pl.ds(LEFT_AT[q], LEFT_AT[q + 1] - LEFT_AT[q])
        return pltpu.make_async_remote_copy(
            src_ref=send_l.at[last, tiles],
            dst_ref=recv_r.at[last, tiles],
            send_sem=part_send_l_sem.at[q],
            recv_sem=part_recv_r_sem.at[q],
            device_id=left,
            device_id_type=MESH,
        )

    def right_part(q):
        tiles = pl.ds(RIGHT_AT[q], RIGHT_AT[q + 1] - RIGHT_AT[q])
        return pltpu.make_async_remote_copy(
            src_ref=send_r.at[last, tiles],
            dst_ref=recv_l.at[last, tiles],
            send_sem=part_send_r_sem.at[q],
            recv_sem=part_recv_l_sem.at[q],
            device_id=right,
            device_id_type=MESH,
        )

    def prepare(r):
        spec_load(r).wait()

        def cast_rows(i, acc):
            rows = pl.ds(pl.multiple_of(i * 64, 64), 64)
            block = spec_v[r, rows, :]
            spec_b[rows, lanes(r)] = block.astype(jnp.bfloat16)
            return acc + jnp.sum(block.reshape(8, 8, NY), axis=0)

        acc = lax.fori_loop(0, components // 64, cast_rows, jnp.zeros((8, NY), jnp.float32))
        average = jnp.sum(acc, axis=0, keepdims=True) * (1.0 / components)
        ratio_v[:, lanes(r)] = jnp.broadcast_to(average / (average + 1.0), (8, NY))

    def source(b, pair):
        rows = pl.ds(pl.multiple_of(b * rows_b, rows_b), rows_b)
        columns = slice(pair[0] * NY, (pair[-1] + 1) * NY)
        product = jnp.dot(coup_v[rows, :], spec_b[:, columns], preferred_element_type=jnp.float32)
        for at, r in enumerate(pair):
            nonlin[r, :rows_b] = product[:, lanes(at)]
        grow = by_freq(growth, b)
        damp = by_freq(dissipation, b)
        damps = {r: damp * ratio_v[:, lanes(r)] for r in pair}

        def directions(i, inner):
            for q in range(4):
                d = q * NQ + i
                cosine = trig[d]
                sine = trig[ND + d]
                made = {}
                for r in pair:
                    forcing = jnp.maximum(cosine * wind_v[0, :, lanes(r)] + sine * wind_v[1, :, lanes(r)], 0.0)
                    value = spec_v[r, pl.ds(b * rows_b + d, FB, stride=ND), :]
                    extra = nonlin[r, pl.ds(d, FB, stride=ND), :]
                    value = value + (grow * (forcing * forcing) - damps[r]) * value + 0.25 * extra
                    energy[b, d, r] = value
                    made[r] = value
                if pair == HIGH:
                    pack_right(q, i, b, made)
                else:
                    pack_left(q, i, b, made)
            return inner

        lax.fori_loop(0, NQ, directions, 0, unroll=3)

    def open_with(first, second):
        for r in first:
            spec_load(r).start()
        coup_load(0).start()
        prepare(first[0])
        prepare(first[1])
        coup_load(0).wait()
        for r in second:
            spec_load(r).start()
        source(0, first)

    def go_on_with(first, second):
        send_of(first, 0).start()
        for r in second:
            prepare(r)
        for b in range(1, blocks):
            coup_load(b).start()
        source(0, second)
        send_of(second, 0).start()

        def others(b, carry):
            coup_load(b).wait()
            source(b, first)
            send_of(first, b).start()
            source(b, second)
            send_of(second, b).start()
            return carry

        lax.fori_loop(1, blocks, others, 0)

    def send_of(pair, k):
        return to_left(k) if pair == LOW else to_right(k)

    low_first = jnp.logical_and(lax.rem(c, 2) == 0, c < ncomp - LINE)
    pl.when(low_first)(lambda: open_with(LOW, HIGH))
    pl.when(jnp.logical_not(low_first))(lambda: open_with(HIGH, LOW))

    row0 = lax.rem(c * RB, 8)
    own_mask = [sea_mask[pl.ds(row0 + r, 1), :] for r in range(RB)]
    own_index = [depth_index[pl.ds(row0 + r, 1), :] for r in range(RB)]
    for side, r in ((0, 0), (1, RB - 1)):
        coast_out[side, 0] = jnp.broadcast_to(own_mask[r], (8, NY))
        coast_out[side, 1] = jnp.broadcast_to(own_index[r], (8, NY))

    pl.semaphore_wait(barrier, 2)

    def coast_copy(side):
        return pltpu.make_async_remote_copy(
            src_ref=coast_out.at[side],
            dst_ref=coast_in.at[1 - side],
            send_sem=coast_send_sem.at[side],
            recv_sem=coast_recv_sem.at[1 - side],
            device_id=left if side == 0 else right,
            device_id_type=MESH,
        )

    for side in range(2):
        coast_copy(side).start()

    pl.when(low_first)(lambda: go_on_with(LOW, HIGH))
    pl.when(jnp.logical_not(low_first))(lambda: go_on_with(HIGH, LOW))

    for side in range(2):
        coast_copy(side).wait()
    mask_rows = (
        [coast_in[0, 0, 0:1, :].astype(jnp.float32) * edge_l]
        + [m.astype(jnp.float32) for m in own_mask]
        + [coast_in[1, 0, 0:1, :].astype(jnp.float32) * edge_r]
    )
    index_rows = [coast_in[0, 1, 0:1, :]] + own_index + [coast_in[1, 1, 0:1, :]]
    levels = depths.shape[0]
    level = lax.broadcasted_iota(jnp.int32, (levels, NY), 0)
    onehot = jnp.concatenate(
        [(jnp.broadcast_to(row, (levels, NY)) == level).astype(jnp.float32) for row in index_rows], axis=1
    )
    speeds = jnp.dot(
        group_speed[...], onehot, precision=lax.Precision.HIGHEST, preferred_element_type=jnp.float32
    )
    turning = jnp.dot(
        refraction[...],
        onehot[:, NY : (RB + 1) * NY],
        precision=lax.Precision.HIGHEST,
        preferred_element_type=jnp.float32,
    )
    lane_row = lax.broadcasted_iota(jnp.int32, (1, NY), 1)
    heights = []
    for row, mask in zip(index_rows, mask_rows):
        height = jnp.zeros((1, NY), jnp.float32)
        for entry in range(levels):
            height = jnp.where(row == entry, depths[entry], height)
        heights.append(height * mask)
    for j in range(RB + 1):
        pair = 0.5 * (speeds[:, lanes(j)] + speeds[:, lanes(j + 1)])
        gx[j] = pair * (mask_rows[j] * mask_rows[j + 1])
    for r in range(RB):
        mask = mask_rows[r + 1]
        own = speeds[:, lanes(r + 1)]
        beyond = jnp.where(lane_row == NY - 1, 0.0, pltpu.roll(jnp.broadcast_to(mask, (8, NY)), NY - 1, 1)[:1])
        gy[r] = 0.5 * (own + pltpu.roll(own, NY - 1, 1)) * (mask * beyond)
        wide = jnp.broadcast_to(heights[r + 1], (8, NY))
        up = jnp.where(lane_row == NY - 1, 0.0, pltpu.roll(wide, NY - 1, 1)[:1])
        down = jnp.where(lane_row == 0, 0.0, pltpu.roll(wide, 1, 1)[:1])
        rx[r] = turning[:, lanes(r)] * (0.5 * (heights[r + 2] - heights[r]))
        ry[r] = turning[:, lanes(r)] * (0.5 * (up - down))
        mask_v[r] = jnp.broadcast_to(mask, (8, NY))


    lane8 = lax.broadcasted_iota(jnp.int32, (FB, NY), 1)
    first_lane = lane8 == 0
    last_lanes = lane8 >= NY - 2

    def turn_face(freqs, d, r, base, diff, second, second_next):
        nu = trig[3 * ND + d] * rx[r, freqs, :] - trig[2 * ND + d] * ry[r, freqs, :]
        return face_of(nu, base, diff, jnp.where(nu >= 0.0, second, second_next))

    def last_passes(freqs, arrive, one_quadrant, emit):
        state = None
        cell = 2
        for q in range(4):
            arrive(q)
            one_quadrant(q)
            if q == 3:
                for d in range(4):
                    for r in range(RB):
                        work[ND + 1 + d, r] = work[1 + d, r]
            if q == 0:
                state = []
                for r in range(RB):
                    e0, e1, e2, e3 = (work[1 + d, r] for d in range(4))
                    d0, d1, d2 = e1 - e0, e2 - e1, e3 - e2
                    face = turn_face(freqs, 1, r, e1, d1, d1 - d0, d2 - d1)
                    state.append((e2, e3, d2, d2 - d1, face))
            until = (q + 1) * NQ - 2 if q < 3 else ND + 2
            while cell < until:
                made = []
                for r in range(RB):
                    e0, e1, diff, second, face_before = state[r]
                    e2 = work[cell + 3, r]
                    diff_next = e2 - e1
                    second_next = diff_next - diff
                    face = turn_face(freqs, cell % ND, r, e0, diff, second, second_next)
                    made.append((e0 - (face - face_before)) * mask_v[r])
                    state[r] = (e1, e2, diff_next, second_next, face)
                emit(None, None, cell % ND, made)
                cell += 1

    def passes(k, b, emit, arrive=None):
        if arrive is None:
            to_left(k).wait_recv()
            to_right(k).wait_recv()
        freqs = pl.ds(pl.multiple_of(b * FB, FB), FB)

        def x_and_y(q, i):
            d = q * NQ + i
            cosine = trig[d]
            sine = trig[ND + d]
            own = [energy[b, d, r] for r in range(RB)]
            low, high = RIGHT_AT[q], LEFT_AT[q]
            if q in (0, 3):
                ext = [recv_l[k, low + 2 * i] * edge_l, recv_l[k, low + 2 * i + 1] * edge_l]
                ext = ext + own + [recv_r[k, high + i] * edge_r]
                shift = 1
            else:
                ext = [recv_l[k, low + i] * edge_l] + own
                ext = ext + [recv_r[k, high + 2 * i] * edge_r, recv_r[k, high + 2 * i + 1] * edge_r]
                shift = 0
            diff = [ext[j + 1] - ext[j] for j in range(RB + 2)]
            second = [diff[j + 1] - diff[j] for j in range(RB + 1)]
            faces = []
            for j in range(RB + 1):
                nu = cosine * gx[j, freqs, :]
                faces.append(face_of(nu, ext[j + shift], diff[j + shift], second[j]))
            for r in range(RB):
                value = own[r] - (faces[r + 1] - faces[r])
                nu = sine * gy[r, freqs, :]
                if q in (0, 1):
                    behind = value - jnp.where(first_lane, 0.0, pltpu.roll(value, 1, 1))
                    ahead = pltpu.roll(value, NY - 1, 1) - value
                    face = face_of(nu, value, ahead, ahead - behind)
                else:
                    next1 = pltpu.roll(value, NY - 1, 1)
                    next2 = jnp.where(last_lanes, 0.0, pltpu.roll(value, NY - 2, 1))
                    ahead = next1 - value
                    face = face_of(nu, value, ahead, next2 - next1 - ahead)
                work[d + 1, r] = value - (face - pltpu.roll(face, 1, 1))

        def along_x_and_y(i, carry):
            for q in range(4):
                x_and_y(q, i)
            return carry

        def one_quadrant(q):
            def run(i, carry):
                x_and_y(q, i)
                return carry

            lax.fori_loop(0, NQ, run, 0, unroll=NQ)

        if arrive is not None:
            last_passes(freqs, arrive, one_quadrant, emit)
            return
        lax.fori_loop(0, NQ, along_x_and_y, 0, unroll=3)
        for r in range(RB):
            work[0, r] = work[ND, r]
            work[ND + 1, r] = work[1, r]
            work[ND + 2, r] = work[2, r]

        carry = []
        for r in range(RB):
            e34, e35, e0, e1 = work[ND - 1, r], work[ND, r], work[1, r], work[2, r]
            d34, d35, d0 = e35 - e34, e0 - e35, e1 - e0
            face = turn_face(freqs, ND - 1, r, e35, d35, d35 - d34, d0 - d35)
            carry.append((e0, e1, d0, d0 - d35, face))
        carry = tuple(carry)
        for q in range(4):

            def along_directions(i, state, q=q):
                d = q * NQ + i
                made = []
                later = []
                for r in range(RB):
                    e0, e1, diff, second, face_before = state[r]
                    e2 = work[d + 3, r]
                    diff_next = e2 - e1
                    second_next = diff_next - diff
                    face = turn_face(freqs, d, r, e0, diff, second, second_next)
                    made.append((e0 - (face - face_before)) * mask_v[r])
                    later.append((e1, e2, diff_next, second_next, face))
                emit(q, i, d, made)
                return tuple(later)

            carry = lax.fori_loop(0, NQ, along_directions, carry, unroll=NQ)

    def middle(k, carry):
        b = lax.rem(k, blocks)

        def emit(q, i, d, rows):
            for r in range(RB):
                energy[b, d, r] = rows[r]
            pack_right(q, i, k + blocks, rows)
            pack_left(q, i, k + blocks, rows)

        passes(k, b, emit)

        @pl.when(jnp.logical_and(k + blocks < last, lax.rem(c, 2) == 0))
        def _():
            to_right(k + blocks).start()
            to_left(k + blocks).start()

        @pl.when(jnp.logical_and(k + blocks < last, lax.rem(c, 2) == 1))
        def _():
            to_left(k + blocks).start()
            to_right(k + blocks).start()

        @pl.when(k + blocks == last)
        def _():
            for q in range(4):
                right_part(q).start()
                left_part(q).start()

        return carry

    lax.fori_loop(0, (SUBSTEPS - 1) * blocks, middle, 0)

    def emit_out(b):
        def emit(q, i, d, rows):
            for r in range(RB):
                out[r, pl.ds(b * rows_b + d, FB, stride=ND), :] = rows[r]

        return emit

    def final(b, carry):
        passes(b + (SUBSTEPS - 1) * blocks, b, emit_out(b))
        return carry

    def arrive(q):
        left_part(q).wait_recv()
        right_part(q).wait_recv()

    lax.fori_loop(0, blocks - 1, final, 0)
    passes(last, blocks - 1, emit_out(blocks - 1), arrive)

    def drain(k, carry):
        to_left(k).wait_send()
        to_right(k).wait_send()
        return carry

    lax.fori_loop(0, last, drain, 0)
    for q in range(4):
        left_part(q).wait_send()
        right_part(q).wait_send()


def hand_on(moved, out, sems):
    chunks = sems.shape[1]
    rows = out.shape[0] // chunks
    copies = [
        pltpu.make_async_copy(
            moved.at[r, pl.ds(j * rows, rows)],
            out.at[pl.ds(j * rows, rows), r * NY : (r + 1) * NY],
            sems.at[r, j],
        )
        for r in range(RB)
        for j in range(chunks)
    ]
    for copy in copies:
        copy.start()
    for copy in copies:
        copy.wait()


def per_device(
    ncomp,
    nspace,
    spectrum,
    wind_field,
    coupling,
    growth,
    dissipation,
    group_speed,
    refraction,
    depths,
    sea_mask,
    depth_index,
):
    nfreq = growth.shape[0]
    blocks = nfreq // FB
    messages = SUBSTEPS * blocks
    components, points = spectrum.shape
    f32 = jnp.float32
    hbm = pl.BlockSpec(memory_space=pl.ANY)
    dma = pltpu.SemaphoreType.DMA
    moved = pl.pallas_call(
        functools.partial(kernel, nfreq, ncomp, nspace),
        out_shape=pltpu.VMEM((RB, components + SPARE, NY), f32),
        in_specs=[hbm] * 10,
        out_specs=pl.BlockSpec(memory_space=pltpu.VMEM),
        scratch_shapes=[
            pltpu.SMEM((4 * ND,), f32),
            pltpu.SMEM(growth.shape, f32),
            pltpu.SMEM(dissipation.shape, f32),
            pltpu.SMEM(depths.shape, f32),
            pltpu.VMEM(wind_field.shape, f32),
            pltpu.VMEM(group_speed.shape, f32),
            pltpu.VMEM(refraction.shape, f32),
            pltpu.VMEM((8, NY), jnp.int32),
            pltpu.VMEM((8, NY), jnp.int32),
            pltpu.VMEM((RB, components + SPARE, NY), f32),
            pltpu.VMEM((components, components), jnp.bfloat16),
            pltpu.VMEM((components, points), jnp.bfloat16),
            pltpu.VMEM((RB, FB * ND + SPARE, NY), f32),
            pltpu.VMEM((blocks, ND, RB, FB, NY), f32),
            pltpu.VMEM((ND + 5, RB, FB, NY), f32),
            pltpu.VMEM((messages, SLOTS, FB, NY), f32),
            pltpu.VMEM((messages, SLOTS, FB, NY), f32),
            pltpu.VMEM((messages, SLOTS, FB, NY), f32),
            pltpu.VMEM((messages, SLOTS, FB, NY), f32),
            pltpu.VMEM((2, 2, 8, NY), jnp.int32),
            pltpu.VMEM((2, 2, 8, NY), jnp.int32),
            pltpu.VMEM((RB + 1, nfreq, NY), f32),
            pltpu.VMEM((RB, nfreq, NY), f32),
            pltpu.VMEM((RB, nfreq, NY), f32),
            pltpu.VMEM((RB, nfreq, NY), f32),
            pltpu.VMEM((RB, 8, NY), f32),
            pltpu.VMEM((2, 8, points), f32),
            pltpu.VMEM((8, points), f32),
            dma((8,)),
            dma((RB,)),
            dma((blocks,)),
            dma((messages,)),
            dma((messages,)),
            dma((messages,)),
            dma((messages,)),
            dma((4,)),
            dma((4,)),
            dma((4,)),
            dma((4,)),
            dma((2,)),
            dma((2,)),
        ],
        compiler_params=pltpu.CompilerParams(
            collective_id=0, has_side_effects=True, vmem_limit_bytes=48 * 1024 * 1024
        ),
    )(
        *[
            pltpu.with_memory_space_constraint(operand, pltpu.HBM)
            for operand in (
                spectrum,
                wind_field,
                coupling,
                growth,
                dissipation,
                group_speed,
                refraction,
                depths,
                sea_mask,
                depth_index,
            )
        ]
    )
    return pl.pallas_call(
        hand_on,
        out_shape=jax.ShapeDtypeStruct((components, points), f32),
        in_specs=[pl.BlockSpec(memory_space=pltpu.VMEM)],
        out_specs=hbm,
        scratch_shapes=[dma((RB, 1))],
    )(pltpu.with_memory_space_constraint(moved, pltpu.VMEM))


def solution(mesh):
    in_specs = (
        P(None, ("comp", "space")),
        P(None, ("comp", "space")),
        P(),
        P(),
        P(),
        P(),
        P(),
        P(),
        P("space", None),
        P("space", None),
    )
    out_specs = P(None, ("comp", "space"))
    body = functools.partial(per_device, mesh.shape["comp"], mesh.shape["space"])
    return jax.shard_map(body, mesh=mesh, in_specs=in_specs, out_specs=out_specs, check_vma=False)
```
